512 devices in a mesh: row: 32 (over x, z), col: 16 (over y, core).
Axes of the slice: x: 4, y: 8, z: 8, core: 2. Of those that a mesh axis runs over, the one named last changes fastest.
Arguments:
- tiles: bfloat16 [32, 16, 64, 128, 128], P('row', 'col'), may hold values from -0.25 to 0.25
- tile_rows: int32 [32, 16, 64], P('row', 'col'), may hold values from 0 to 127
- tile_cols: int32 [32, 16, 64], P('row', 'col'), may hold values from 0 to 255
- tile_count: int32 [32, 16], P('row', 'col'), may hold values from 1 to 64, as said below
- cost: float32 [524288], P('col'), may hold values from -12 to 12
- upper: float32 [524288], P('col'), may hold values from 0.3 to 4
- var_kind: int32 [524288], P('col'), may hold values from 0 to 2
- rhs: float32 [524288], P('row'), may hold values from -12 to 12
- row_kind: int32 [524288], P('row'), may hold values from 0 to 1
- primal_start: float32 [524288], P('col'), may hold values from -6 to 6
- dual_start: float32 [524288], P('row'), may hold values from -6 to 6
Outputs:
- primal: float32 [524288], P(('col', 'row'))
- dual: float32 [524288], P(('row', 'col'))
- primal_avg: float32 [524288], P(('col', 'row'))
- dual_avg: float32 [524288], P(('row', 'col'))
- objectives: float32 [2], replicated
The draws below stay inside these ranges and needn't reach their ends.
Inputs may be any that keep to these rules, and one draw needn't show every extreme that they name: `tile_count`: at most 64 live slots on a device; some device has exactly 64.
All inputs are finite; a program needn't handle non-finite values.
Results may differ from the reference program's by a relative error of at most 0.0012.
Values may be sent and summed in bfloat16 or wider, within the bound.
A program may use at most 64 MiB of HBM per device.

```python
import math
import jax
import jax.numpy as jnp
from jax import lax

TILE = 128
RB = 128
CB = 256
TILES_DEV = 64
ITERS = 2
NROWS = 524288
NCOLS = 524288
N_ROW = 32
N_COL = 16


def draw_tile_count(key, part):
    key = jax.random.fold_in(key, 11)
    first_key, second_key, third_key = jax.random.split(key, 3)
    first = jax.random.randint(first_key, (N_ROW * N_COL,), 1, TILES_DEV + 1)
    second = jax.random.randint(second_key, (N_ROW * N_COL,), 1, TILES_DEV + 1)
    counts = jnp.minimum(first, second)
    chosen = jax.random.randint(third_key, (), 0, N_ROW * N_COL)
    counts = jnp.where(jnp.arange(N_ROW * N_COL) == chosen, TILES_DEV, counts)
    return counts.reshape(N_ROW, N_COL).astype(jnp.int32)


def draw_cost(key, part):
    key = jax.random.fold_in(key, 21)
    ramp = 1.0 + 2.0 * jnp.arange(NCOLS, dtype=jnp.float32) / (NCOLS - 1)
    values = jnp.clip(jax.random.normal(key, (NCOLS,), jnp.float32), -4.0, 4.0) * ramp
    return values.astype(jnp.float32)


def draw_rhs(key, part):
    key = jax.random.fold_in(key, 31)
    ramp = 1.0 + 2.0 * jnp.arange(NROWS, dtype=jnp.float32) / (NROWS - 1)
    values = jnp.clip(jax.random.normal(key, (NROWS,), jnp.float32), -4.0, 4.0) * ramp
    return values.astype(jnp.float32)


def set_ends(entries, rng, low, largest):
    extent = entries.shape
    index_at = [jax.random.randint(jax.random.fold_in(rng, axis), (), 0, extent[axis]) for axis in range(len(extent))]
    entries = entries.at[tuple(index_at)].set(low)
    longest = extent.index(max(extent))
    index_at[longest] = (index_at[longest] + 1) % extent[longest]
    return entries.at[tuple(index_at)].set(largest)


def block_levels(rng, extent, shards, least, top_value):
    factor_of, own = 1.0, jax.random.fold_in(rng, 6)
    for dim, shards_of in shards:
        heights = jnp.exp(jax.random.uniform(jax.random.fold_in(own, dim), (shards_of,), jnp.float32, least / len(shards), top_value / len(shards)))
        factor_of = factor_of * jnp.repeat(heights, extent[dim] // shards_of).reshape([-1 if axis == dim else 1 for axis in range(len(extent))])
    return factor_of


def gaussian(own_key, shape, scale, limit, cuts=(), kind=jnp.bfloat16):
    factor_of = block_levels(own_key, shape, cuts, -0.22, 0.18) if cuts else 1.0
    drawn = jax.random.normal(own_key, shape, jnp.float32) * scale * factor_of
    return jnp.minimum(jnp.maximum(drawn, -limit), limit).astype(kind)


def setup_inputs(seed: int = 0) -> dict:
    splits = jax.random.split(jax.random.key(seed), 12)
    return {
        "tiles": gaussian(splits[0], (N_ROW, N_COL, TILES_DEV, TILE, TILE), 512 ** -0.5, 0.25, ((0, 32), (1, 16))),
        "tile_rows": set_ends(jax.random.randint(splits[1], (N_ROW, N_COL, TILES_DEV), 0, RB), jax.random.fold_in(splits[1], 1), 0, RB - 1).astype(jnp.int32),
        "tile_cols": set_ends(jax.random.randint(splits[2], (N_ROW, N_COL, TILES_DEV), 0, CB), jax.random.fold_in(splits[2], 1), 0, CB - 1).astype(jnp.int32),
        "tile_count": draw_tile_count(jax.random.fold_in(splits[11], 71), 0),
        "cost": draw_cost(jax.random.fold_in(splits[11], 71), 0),
        "upper": jnp.clip(jnp.exp(math.log(4.0) - 2.5902671 * jax.random.uniform(splits[5], (NCOLS,), jnp.float32) ** block_levels(splits[5], (NCOLS,), ((0, 16),), -0.2, 0.2)), 0.3, 4.0),
        "var_kind": set_ends(jax.random.randint(splits[6], (NCOLS,), 0, 3), jax.random.fold_in(splits[6], 1), 0, 2).astype(jnp.int32),
        "rhs": draw_rhs(jax.random.fold_in(splits[11], 71), 0),
        "row_kind": set_ends(jax.random.randint(splits[8], (NROWS,), 0, 2), jax.random.fold_in(splits[8], 1), 0, 1).astype(jnp.int32),
        "primal_start": gaussian(splits[9], (NCOLS,), 1.0, 6.0, ((0, 16),), jnp.float32),
        "dual_start": gaussian(splits[10], (NROWS,), 1.0, 6.0, ((0, 32),), jnp.float32),
    }


primal_step = 0.4
dual_step = 0.4

def project_primal(value, var_kind, upper):
    lower_cut = jnp.where(var_kind == 2, value, jnp.maximum(value, 0.0))
    return jnp.where(var_kind == 0, jnp.minimum(lower_cut, upper), lower_cut)

def project_dual(value, row_kind):
    return jnp.where(row_kind == 1, jnp.maximum(value, 0.0), value)

def reference(tiles, tile_rows, tile_cols, tile_count, cost, upper, var_kind, rhs, row_kind, primal_start, dual_start):
    pairs = N_ROW * N_COL
    slots = jnp.arange(TILES_DEV, dtype=jnp.int32)
    live_mask = (slots[None, None, :] < tile_count[:, :, None]).astype(jnp.float32).reshape(pairs, TILES_DEV, 1)
    global_rows = (jnp.arange(N_ROW, dtype=jnp.int32)[:, None, None] * RB + tile_rows).reshape(-1).astype(jnp.int32)
    global_cols = (jnp.arange(N_COL, dtype=jnp.int32)[None, :, None] * CB + tile_cols).reshape(-1).astype(jnp.int32)
    flat_tiles = tiles.reshape(pairs, TILES_DEV, TILE, TILE)

    def apply_forward(vector):
        blocks = vector.reshape(-1, TILE)[global_cols].reshape(pairs, TILES_DEV, TILE)

        def one_pair(items):
            return jnp.einsum('tij,tj->ti', items[0].astype(jnp.float32), items[1].astype(jnp.float32)) * items[2]
        products = lax.map(one_pair, (flat_tiles, blocks, live_mask))
        total = jnp.zeros((NROWS // TILE, TILE), jnp.float32).at[global_rows].add(products.reshape(-1, TILE))
        return total.reshape(-1)

    def apply_backward(vector):
        blocks = vector.reshape(-1, TILE)[global_rows].reshape(pairs, TILES_DEV, TILE)

        def one_pair(items):
            return jnp.einsum('tij,ti->tj', items[0].astype(jnp.float32), items[1].astype(jnp.float32)) * items[2]
        products = lax.map(one_pair, (flat_tiles, blocks, live_mask))
        total = jnp.zeros((NCOLS // TILE, TILE), jnp.float32).at[global_cols].add(products.reshape(-1, TILE))
        return total.reshape(-1)
    primal_now = primal_start
    dual_now = dual_start
    primal_total = jnp.zeros_like(primal_start)
    dual_total = jnp.zeros_like(dual_start)
    for step in range(ITERS):
        dual_image = apply_backward(dual_now.astype(jnp.bfloat16))
        primal_next = project_primal(primal_now - primal_step * (cost - dual_image), var_kind, upper)
        extrapolated = (2.0 * primal_next - primal_now).astype(jnp.bfloat16)
        primal_image = apply_forward(extrapolated)
        dual_next = project_dual(dual_now + dual_step * (rhs - primal_image), row_kind)
        primal_now, dual_now = (primal_next, dual_next)
        primal_total = primal_total + primal_next
        dual_total = dual_total + dual_next
    primal_avg = primal_total / ITERS
    dual_avg = dual_total / ITERS
    objectives = jnp.stack([jnp.sum(cost * primal_avg) / math.sqrt(NCOLS), jnp.sum(rhs * dual_avg) / math.sqrt(NROWS)])
    return (primal_now, dual_now, primal_avg, dual_avg, objectives)
```

```python
import functools
import math

import jax
import jax.numpy as jnp
from jax import lax
from jax.experimental import pallas as pl
from jax.experimental.pallas import tpu as pltpu
from jax.sharding import PartitionSpec as P

MESH = pl.DeviceIdType.MESH
TILE = 128
SHARE = 8
GROUP = 16
ITERS = 2
SEND = jnp.bfloat16
PRIMAL_STEP = 0.4
DUAL_STEP = 0.4
BF16 = jnp.bfloat16
F32 = jnp.float32


def project_primal(value, var_kind, upper):
    lower_cut = jnp.where(var_kind == 2, value, jnp.maximum(value, 0.0))
    return jnp.where(var_kind == 0, jnp.minimum(lower_cut, upper), lower_cut)


def project_dual(value, row_kind):
    return jnp.where(row_kind == 1, jnp.maximum(value, 0.0), value)


def zigzag(step, size):
    half = lax.div(step + 1, 2)
    return size // 2 + jnp.where(lax.rem(step, 2) == 0, half, -half)


def split_dot(onehot, products):
    high = products.astype(BF16)
    low = (products - high.astype(F32)).astype(BF16)
    return jnp.dot(onehot, high, preferred_element_type=F32) + jnp.dot(
        onehot, low, preferred_element_type=F32
    )


def kernel(
    sizes,
    tiles_hbm,
    trow_ref,
    tcol_ref,
    count_ref,
    cost_hbm,
    upper_hbm,
    kind_hbm,
    rhs_hbm,
    rkind_hbm,
    primal_hbm,
    dual_hbm,
    out_ref,
    tiles,
    dual_full,
    vecs,
    kinds,
    rs_row_src,
    rs_row_dst,
    ag_row_src,
    ag_row_dst,
    rs_col_src,
    rs_col_dst,
    ag_col_src,
    ag_col_dst,
    obj_col_src,
    obj_col_dst,
    obj_row_src,
    obj_row_dst,
    load_sems,
    send_sems,
    recv_sems,
):
    n_x, n_z, n_y, n_core, slots = sizes
    n_row, n_col = n_x * n_z, n_y * n_core
    me_row = lax.axis_index("row")
    me_col = lax.axis_index("col")
    my_x, my_z = lax.div(me_row, n_z), lax.rem(me_row, n_z)
    my_y, my_core = lax.div(me_col, n_core), lax.rem(me_col, n_core)

    def row_peer(step):
        dz = zigzag(lax.div(step, n_x), n_z)
        dx = zigzag(lax.rem(step, n_x), n_x)
        return lax.rem(my_x + dx, n_x) * n_z + lax.rem(my_z + dz, n_z)

    def col_peer(step):
        dy = zigzag(lax.div(step, n_core), n_y)
        dcore = n_core - 1 - lax.rem(step, n_core)
        return lax.rem(my_y + dy, n_y) * n_core + lax.rem(my_core + dcore, n_core)

    barrier = pltpu.get_barrier_semaphore()

    @pl.loop(0, n_row - 1)
    def _(step):
        pl.semaphore_signal(
            barrier, inc=1, device_id={"row": row_peer(step)}, device_id_type=MESH
        )

    @pl.loop(0, n_col - 1)
    def _(step):
        pl.semaphore_signal(
            barrier, inc=1, device_id={"col": col_peer(step)}, device_id_type=MESH
        )

    row_share = pl.ds(pl.multiple_of(me_row * SHARE, SHARE), SHARE)
    col_share = pl.ds(pl.multiple_of(me_col * SHARE, SHARE), SHARE)
    loads = [
        pltpu.make_async_copy(dual_hbm, dual_full, load_sems.at[0]),
        pltpu.make_async_copy(tiles_hbm, tiles, load_sems.at[1]),
        pltpu.make_async_copy(cost_hbm.at[row_share], vecs.at[0], load_sems.at[2]),
        pltpu.make_async_copy(upper_hbm.at[row_share], vecs.at[1], load_sems.at[3]),
        pltpu.make_async_copy(primal_hbm.at[row_share], vecs.at[2], load_sems.at[4]),
        pltpu.make_async_copy(rhs_hbm.at[col_share], vecs.at[3], load_sems.at[5]),
        pltpu.make_async_copy(dual_hbm.at[col_share], vecs.at[4], load_sems.at[6]),
        pltpu.make_async_copy(kind_hbm.at[row_share], kinds.at[0], load_sems.at[7]),
        pltpu.make_async_copy(rkind_hbm.at[col_share], kinds.at[1], load_sems.at[8]),
    ]
    for load in loads:
        load.start()

    n_rblocks, n_cblocks = n_col * SHARE, n_row * SHARE
    live = lax.broadcasted_iota(jnp.int32, (1, slots), 1) < count_ref[0, 0]
    block_rows = jnp.where(live, trow_ref[...], -1)
    block_cols = jnp.where(live, tcol_ref[...], -1)
    row_hot = (
        lax.broadcasted_iota(jnp.int32, (n_rblocks, slots), 0) == block_rows
    ).astype(F32)
    col_hot = (
        lax.broadcasted_iota(jnp.int32, (n_cblocks, slots), 0) == block_cols
    ).astype(F32)
    row_pick, col_pick = row_hot.T.astype(BF16), col_hot.T.astype(BF16)
    row_put, col_put = row_hot.astype(BF16), col_hot.astype(BF16)
    sub = lax.broadcasted_iota(jnp.int32, (GROUP, TILE), 0)

    def back(dual_wide):
        picked = jnp.dot(row_pick, dual_wide, preferred_element_type=F32)
        products = []
        for g in range(slots // GROUP):
            part = picked[g * GROUP : (g + 1) * GROUP]
            spread = jnp.concatenate(
                [jnp.where(sub == j, part, 0.0).astype(BF16) for j in range(GROUP)], axis=1
            )
            block = tiles[g * GROUP : (g + 1) * GROUP].reshape(GROUP * TILE, TILE)
            products.append(jnp.dot(spread, block, preferred_element_type=F32))
        return split_dot(col_put, jnp.concatenate(products, axis=0))

    def fore(primal_wide):
        picked = jnp.dot(col_pick, primal_wide, preferred_element_type=F32).astype(BF16)
        products = []
        for g in range(slots // GROUP):
            part = picked[g * GROUP : (g + 1) * GROUP]
            block = tiles[g * GROUP : (g + 1) * GROUP].reshape(GROUP * TILE, TILE)
            every = lax.dot_general(
                part, block, (((1,), (1,)), ((), ())), preferred_element_type=F32
            )
            own = jnp.zeros((GROUP, TILE), F32)
            for j in range(GROUP):
                own = own + jnp.where(sub == j, every[:, j * TILE : (j + 1) * TILE], 0.0)
            products.append(own)
        return split_dot(row_put, jnp.concatenate(products, axis=0))

    pending = []

    def exchange(axis, phase, source, dest, scatter):
        n, me, peer_of = (
            (n_row, me_row, row_peer) if axis == "row" else (n_col, me_col, col_peer)
        )

        @pl.loop(0, n - 1)
        def _(step):
            peer = peer_of(step)
            pltpu.make_async_remote_copy(
                src_ref=source.at[peer] if scatter else source,
                dst_ref=dest.at[me],
                send_sem=send_sems.at[phase],
                recv_sem=recv_sems.at[phase],
                device_id={axis: peer},
                device_id_type=MESH,
            ).start()

        dest[me] = source[me] if scatter else source[...]
        both = dest.at[pl.ds(0, n - 1)]
        pltpu.make_async_copy(both, both, recv_sems.at[phase]).wait()
        pending.append((both, phase))
        return dest[...]

    for load in loads[:2]:
        load.wait()
    partial = back(dual_full[...].astype(BF16))
    rs_row_src[0] = partial.reshape(n_row, SHARE, TILE).astype(SEND)
    for load in loads[2:]:
        load.wait()
    cost, upper, primal_now, rhs, dual_now = (vecs[i] for i in range(5))
    var_kind, row_kind = kinds[0], kinds[1]
    pl.semaphore_wait(barrier, n_row + n_col - 2)

    primal_total = jnp.zeros_like(primal_now)
    dual_total = jnp.zeros_like(dual_now)
    phase = 0
    for it in range(ITERS):
        got = exchange("row", phase, rs_row_src.at[it], rs_row_dst.at[it], True)
        phase += 1
        dual_image = jnp.sum(got.astype(F32), axis=0)
        primal_next = project_primal(
            primal_now - PRIMAL_STEP * (cost - dual_image), var_kind, upper
        )
        ag_row_src[it] = (2.0 * primal_next - primal_now).astype(BF16)
        got = exchange("row", phase, ag_row_src.at[it], ag_row_dst.at[it], False)
        phase += 1
        wide = got.astype(F32).reshape(n_cblocks, TILE).astype(BF16)
        rs_col_src[it] = fore(wide).reshape(n_col, SHARE, TILE).astype(SEND)
        got = exchange("col", phase, rs_col_src.at[it], rs_col_dst.at[it], True)
        phase += 1
        primal_image = jnp.sum(got.astype(F32), axis=0)
        dual_next = project_dual(dual_now + DUAL_STEP * (rhs - primal_image), row_kind)
        primal_now, dual_now = primal_next, dual_next
        primal_total = primal_total + primal_next
        dual_total = dual_total + dual_next
        if it + 1 < ITERS:
            ag_col_src[it] = dual_next.astype(BF16)
            got = exchange("col", phase, ag_col_src.at[it], ag_col_dst.at[it], False)
            phase += 1
            wide = got.astype(F32).reshape(n_rblocks, TILE).astype(BF16)
            rs_row_src[it + 1] = back(wide).reshape(n_row, SHARE, TILE).astype(SEND)

    primal_avg, dual_avg = primal_total / ITERS, dual_total / ITERS
    obj_col_src[0:1] = jnp.sum(cost * primal_avg, axis=0, keepdims=True)
    obj_col_src[1:2] = jnp.sum(rhs * dual_avg, axis=0, keepdims=True)
    got = exchange("col", phase, obj_col_src, obj_col_dst, False)
    phase += 1
    obj_row_src[...] = jnp.sum(got, axis=0)
    got = exchange("row", phase, obj_row_src, obj_row_dst, False)
    inner = jnp.sum(jnp.sum(got, axis=0), axis=1, keepdims=True)
    primal_scale = 1.0 / math.sqrt(n_cblocks * TILE * n_col)
    dual_scale = 1.0 / math.sqrt(n_rblocks * TILE * n_row)
    first = lax.broadcasted_iota(jnp.int32, (SHARE, TILE), 1) == 0
    out_ref[0] = primal_now
    out_ref[1] = dual_now
    out_ref[2] = primal_avg
    out_ref[3] = dual_avg
    out_ref[4] = jnp.where(first, inner[0:1] * primal_scale, inner[1:2] * dual_scale)
    for both, which in pending:
        pltpu.make_async_copy(both, both, send_sems.at[which]).wait()


def split_kernel(packed_ref, *out_refs):
    for i in range(4):
        out_refs[i][...] = packed_ref[i]
    out_refs[4][...] = packed_ref[4]


def solution(mesh):
    n_row, n_col = mesh.shape["row"], mesh.shape["col"]
    n_x, n_core = 4, 2
    n_z, n_y = n_row // n_x, n_col // n_core

    def body(
        tiles,
        tile_rows,
        tile_cols,
        tile_count,
        cost,
        upper,
        var_kind,
        rhs,
        row_kind,
        primal_start,
        dual_start,
    ):
        slots = tiles.shape[2]
        sizes = (n_x, n_z, n_y, n_core, slots)
        n_rblocks, n_cblocks = n_col * SHARE, n_row * SHARE
        anywhere = pl.BlockSpec(memory_space=pl.ANY)
        vmem = pl.BlockSpec(memory_space=pltpu.VMEM)
        smem = pl.BlockSpec(memory_space=pltpu.SMEM)
        n_phases = 4 * ITERS + 1
        packed = pl.pallas_call(
            functools.partial(kernel, sizes),
            out_shape=jax.ShapeDtypeStruct((5, SHARE, TILE), F32),
            in_specs=[anywhere, vmem, vmem, smem] + [anywhere] * 7,
            out_specs=vmem,
            scratch_shapes=[
                pltpu.VMEM((slots, TILE, TILE), BF16),
                pltpu.VMEM((n_rblocks, TILE), F32),
                pltpu.VMEM((5, SHARE, TILE), F32),
                pltpu.VMEM((2, SHARE, TILE), jnp.int32),
                pltpu.VMEM((ITERS, n_row, SHARE, TILE), SEND),
                pltpu.VMEM((ITERS, n_row, SHARE, TILE), SEND),
                pltpu.VMEM((ITERS, SHARE, TILE), BF16),
                pltpu.VMEM((ITERS, n_row, SHARE, TILE), BF16),
                pltpu.VMEM((ITERS, n_col, SHARE, TILE), SEND),
                pltpu.VMEM((ITERS, n_col, SHARE, TILE), SEND),
                pltpu.VMEM((ITERS - 1, SHARE, TILE), BF16),
                pltpu.VMEM((ITERS - 1, n_col, SHARE, TILE), BF16),
                pltpu.VMEM((2, TILE), F32),
                pltpu.VMEM((n_col, 2, TILE), F32),
                pltpu.VMEM((2, TILE), F32),
                pltpu.VMEM((n_row, 2, TILE), F32),
                pltpu.SemaphoreType.DMA((9,)),
                pltpu.SemaphoreType.DMA((n_phases,)),
                pltpu.SemaphoreType.DMA((n_phases,)),
            ],
            compiler_params=pltpu.CompilerParams(
                collective_id=0, has_side_effects=True, vmem_limit_bytes=60 * 2**20
            ),
            name="pdhg",
        )(
            tiles.reshape(slots, TILE, TILE),
            tile_rows.reshape(1, slots),
            tile_cols.reshape(1, slots),
            tile_count,
            cost.reshape(n_cblocks, TILE),
            upper.reshape(n_cblocks, TILE),
            var_kind.reshape(n_cblocks, TILE),
            rhs.reshape(n_rblocks, TILE),
            row_kind.reshape(n_rblocks, TILE),
            primal_start.reshape(n_cblocks, TILE),
            dual_start.reshape(n_rblocks, TILE),
        )
        share = jax.ShapeDtypeStruct((SHARE, TILE), F32)
        outs = pl.pallas_call(
            split_kernel,
            out_shape=(share,) * 5,
            in_specs=[vmem],
            out_specs=(vmem,) * 5,
            name="unpack",
        )(packed)
        return tuple(o.reshape(-1) for o in outs[:4]) + (outs[4][0, :2],)

    placed = (
        P("row", "col", None, None, None),
        P("row", "col", None),
        P("row", "col", None),
        P("row", "col"),
        P("col"),
        P("col"),
        P("col"),
        P("row"),
        P("row"),
        P("col"),
        P("row"),
    )
    return jax.shard_map(
        body,
        mesh=mesh,
        in_specs=placed,
        out_specs=(P(("col", "row")), P(("row", "col")), P(("col", "row")), P(("row", "col")), P()),
        check_vma=False,
    )
```

```python
import functools
import math

import jax
import jax.numpy as jnp
from jax import lax
from jax.experimental import pallas as pl
from jax.experimental.pallas import tpu as pltpu
from jax.sharding import PartitionSpec as P

MESH = pl.DeviceIdType.MESH
TILE = 128
SHARE = 8
GROUP = 16
ITERS = 2
N_X = 4
N_CORE = 2
LEVELS = 32767.0
PRIMAL_STEP = 0.4
DUAL_STEP = 0.4
BF16 = jnp.bfloat16
F32 = jnp.float32
I32 = jnp.int32
I16 = jnp.int16
SEMS = 24


def project_primal(value, var_kind, upper):
    lower_cut = jnp.where(var_kind == 2, value, jnp.maximum(value, 0.0))
    return jnp.where(var_kind == 0, jnp.minimum(lower_cut, upper), lower_cut)


def project_dual(value, row_kind):
    return jnp.where(row_kind == 1, jnp.maximum(value, 0.0), value)


def zigzag(step, size):
    half = lax.div(step + 1, 2)
    return size // 2 + jnp.where(lax.rem(step, 2) == 0, half, -half)


def twice(row):
    wide = jnp.broadcast_to(row, (8, TILE))
    lane = lax.broadcasted_iota(I32, wide.shape, 1)
    return jnp.where(lane < TILE // 2, wide, pltpu.roll(wide, TILE // 2, 1))


def quantize(sums):
    top = jnp.max(jnp.abs(sums), axis=-2, keepdims=True)
    inverse = LEVELS / jnp.maximum(top, 1e-30)
    return jnp.round(sums * inverse).astype(I32).astype(I16), top * (1.0 / LEVELS)


def kernel(
    sizes,
    tiles_hbm,
    trow_hbm,
    tcol_hbm,
    count_ref,
    cost_hbm,
    upper_hbm,
    kind_hbm,
    rhs_hbm,
    rkind_hbm,
    primal_hbm,
    dual_hbm,
    out_ref,
    tiles,
    raw_idx,
    col_vecs,
    col_kind,
    row_vecs,
    row_kind_full,
    idx_src,
    idx_x,
    idx_z,
    idx_y,
    idx_c,
    match_z,
    match_y,
    px_src,
    px_dst,
    zq_src,
    zq_dst,
    zs_src,
    zs_dst,
    zo_src,
    zo_dst,
    pc_src,
    pc_dst,
    yq_src,
    yq_dst,
    ys_src,
    ys_dst,
    yo_src,
    yo_dst,
    lq_src,
    ls_src,
    mid_src,
    mid_dst,
    po_src,
    po_dst,
    last_y,
    fin_src,
    fin_dst,
    load_sems,
    send_sems,
    recv_sems,
):
    n_x, n_z, n_y, n_core, slots = sizes
    n_row, n_col = n_x * n_z, n_y * n_core
    n_rblocks, n_cblocks = n_col * SHARE, n_row * SHARE
    me_row = lax.axis_index("row")
    me_col = lax.axis_index("col")
    my_x, my_z = lax.div(me_row, n_z), lax.rem(me_row, n_z)
    my_y, my_core = lax.div(me_col, n_core), lax.rem(me_col, n_core)

    def x_peer(step):
        at = lax.rem(my_x + zigzag(step, n_x), n_x)
        return at, (at * n_z + my_z, me_col)

    def z_peer(step):
        at = lax.rem(my_z + zigzag(step, n_z), n_z)
        return at, (my_x * n_z + at, me_col)

    def y_peer(step):
        at = lax.rem(my_y + zigzag(step, n_y), n_y)
        return at, (me_row, at * n_core + my_core)

    def core_peer(step):
        at = lax.rem(my_core + 1 + step, n_core)
        return at, (me_row, my_y * n_core + at)

    def last_peer(step):
        ahead = lax.div(step, n_core)
        at_z = lax.rem(my_z + zigzag(lax.div(ahead, n_x), n_z), n_z)
        at_x = lax.rem(my_x + zigzag(lax.rem(ahead, n_x), n_x), n_x)
        at_core = lax.rem(my_core + n_core - 1 - lax.rem(step, n_core), n_core)
        return step, (at_x * n_z + at_z, my_y * n_core + at_core)

    barrier = pltpu.get_barrier_semaphore()
    n_last = n_row * n_core

    @pl.loop(0, n_last - 1)
    def _(step):
        pl.semaphore_signal(barrier, inc=1, device_id=last_peer(step)[1], device_id_type=MESH)

    @pl.loop(0, n_y - 1)
    def _(step):
        pl.semaphore_signal(barrier, inc=1, device_id=y_peer(step)[1], device_id_type=MESH)

    n_groups = slots // GROUP
    pieces = [pl.ds(g * GROUP, GROUP) for g in range(n_groups)]
    first_loads = [
        (trow_hbm, raw_idx.at[0]),
        (tcol_hbm, raw_idx.at[1]),
        (dual_hbm, row_vecs.at[0]),
    ]
    tile_loads = [(tiles_hbm.at[piece], tiles.at[piece]) for piece in pieces]
    late_loads = [
        (primal_hbm, col_vecs.at[0]),
        (cost_hbm, col_vecs.at[1]),
        (upper_hbm, col_vecs.at[2]),
        (kind_hbm, col_kind),
        (rhs_hbm, row_vecs.at[1]),
        (rkind_hbm, row_kind_full),
    ]
    copies = [
        pltpu.make_async_copy(src, dst, load_sems.at[i])
        for i, (src, dst) in enumerate(first_loads + tile_loads + late_loads)
    ]
    for copy in copies:
        copy.start()
    n_first, n_tile = len(first_loads), len(tile_loads)
    for copy in copies[:n_first]:
        copy.wait()

    live = lax.broadcasted_iota(I32, (1, slots), 1) < count_ref[0, 0]
    block_rows = jnp.where(live, raw_idx[0], -1)
    block_cols = jnp.where(live, raw_idx[1], -1)
    row_pick = (
        (lax.broadcasted_iota(I32, (n_rblocks, slots), 0) == block_rows).astype(F32).T
    )
    sub = lax.broadcasted_iota(I32, (GROUP, TILE), 0)

    def back(part_of, ready):
        products = []
        for g in range(n_groups):
            ready(g)
            part = part_of[g * GROUP : (g + 1) * GROUP]
            spread = jnp.concatenate(
                [jnp.where(sub == j, part, 0.0).astype(BF16) for j in range(GROUP)], axis=1
            )
            block = tiles[g * GROUP : (g + 1) * GROUP].reshape(GROUP * TILE, TILE)
            products.append(jnp.dot(spread, block, preferred_element_type=F32))
        return jnp.concatenate(products, axis=0)

    def fore(part_of):
        products = []
        for g in range(n_groups):
            part = part_of[g * GROUP : (g + 1) * GROUP]
            block = tiles[g * GROUP : (g + 1) * GROUP].reshape(GROUP * TILE, TILE)
            every = lax.dot_general(
                part, block, (((1,), (1,)), ((), ())), preferred_element_type=F32
            )
            own = jnp.zeros((GROUP, TILE), F32)
            for j in range(GROUP):
                own = own + jnp.where(sub == j, every[:, j * TILE : (j + 1) * TILE], 0.0)
            products.append(own)
        return jnp.concatenate(products, axis=0)

    pending = []
    used = [0]

    def send(peer, count, source, dest, slot):
        sem = used[0]
        used[0] += 1

        @pl.loop(0, count)
        def _(step):
            at, device = peer(step)
            pltpu.make_async_remote_copy(
                src_ref=source(at),
                dst_ref=dest.at[slot],
                send_sem=send_sems.at[sem],
                recv_sem=recv_sems.at[sem],
                device_id=device,
                device_id_type=MESH,
            ).start()

        both = dest.at[pl.ds(0, count)]
        pending.append((both, sem))

        def arrive():
            pltpu.make_async_copy(both, both, recv_sems.at[sem]).wait()

        return arrive

    def put_split(ref, products):
        high = products.astype(BF16)
        ref[0:slots] = high
        ref[slots : 2 * slots] = (products - high.astype(F32)).astype(BF16)

    rounded = row_vecs[0].astype(BF16)
    picked = jnp.dot(row_pick.astype(BF16), rounded, preferred_element_type=F32)
    put_split(px_src.at[0], back(picked, lambda g: copies[n_first + g].wait()))
    idx_src[...] = jnp.full((2, TILE), -1, I32)
    idx_src[0:1, 0:slots] = block_cols
    idx_src[1:2, 0:slots] = block_rows
    pl.semaphore_wait(barrier, n_last - 1 + n_y - 1)

    z_idx_in = send(z_peer, n_z - 1, lambda at: idx_src, idx_z, my_z)
    x_idx_in = send(x_peer, n_x - 1, lambda at: idx_src, idx_x, my_x)
    x_in = send(x_peer, n_x - 1, lambda at: px_src.at[0], px_dst.at[0], my_x)
    y_idx_in = send(y_peer, n_y - 1, lambda at: idx_src, idx_y, my_y)
    c_idx_in = send(core_peer, n_core - 1, lambda at: idx_src, idx_c, my_core)
    for mine, ref in ((my_x, idx_x), (my_z, idx_z), (my_y, idx_y), (my_core, idx_c)):
        ref[mine] = idx_src[...]
    px_dst[0, my_x] = px_src[0]

    for copy in copies[n_first + n_tile :]:
        copy.wait()
    col_pick = (
        (lax.broadcasted_iota(I32, (n_cblocks, slots), 0) == block_cols).astype(F32).T
    )
    col_all = jnp.concatenate(
        [col_vecs[0], col_vecs[1], col_vecs[2], col_kind[...].astype(F32)], axis=1
    )
    col_got = jnp.dot(
        col_pick, col_all, precision=lax.Precision.HIGHEST, preferred_element_type=F32
    )
    x_need, cost_need, upper_need, kind_need = (
        col_got[:, i * TILE : (i + 1) * TILE] for i in range(4)
    )
    row_all = jnp.concatenate(
        [row_vecs[0], row_vecs[1], row_kind_full[...].astype(F32)], axis=1
    )
    row_got = jnp.dot(
        row_pick, row_all, precision=lax.Precision.HIGHEST, preferred_element_type=F32
    )
    y_need, rhs_need, rkind_need = (row_got[:, i * TILE : (i + 1) * TILE] for i in range(3))
    row_share = pl.ds(pl.multiple_of(me_row * SHARE, SHARE), SHARE)
    col_share = pl.ds(pl.multiple_of(me_col * SHARE, SHARE), SHARE)
    x_own, cost_own, upper_own = (col_vecs[i, row_share] for i in range(3))
    kind_own = col_kind[row_share]
    y_own, rhs_own, rkind_own = row_vecs[0, col_share], row_vecs[1, col_share], row_kind_full[col_share]

    z_idx_in()
    x_idx_in()
    need_cols = idx_z[:, 0, :].astype(F32).T[:slots]
    own_cols = lax.broadcasted_iota(I32, (n_z * SHARE, TILE), 0) + my_x * (n_z * SHARE)
    for k in range(n_x):
        have = twice(idx_x[k, 0:1])
        lanes = slice(k * TILE, (k + 1) * TILE)
        have_wide = jnp.broadcast_to(have[0:1], (slots, TILE)).astype(F32)
        for z in range(n_z):
            match_z[z * slots : (z + 1) * slots, lanes] = jnp.where(
                need_cols[:, z : z + 1] == have_wide, 1.0, 0.0
            ).astype(BF16)
        match_z[n_z * slots :, lanes] = jnp.where(own_cols == have[0:1], 1.0, 0.0).astype(BF16)
    y_idx_in()
    c_idx_in()
    need_rows = idx_y[:, 1, :].astype(F32).T[:slots]
    own_at = lax.broadcasted_iota(I32, (n_y * SHARE, TILE), 0)
    own_rows = (lax.div(own_at, SHARE) * n_core + my_core) * SHARE + lax.rem(own_at, SHARE)
    for k in range(n_core):
        have = twice(idx_c[k, 1:2])
        lanes = slice(k * TILE, (k + 1) * TILE)
        have_wide = jnp.broadcast_to(have[0:1], (slots, TILE)).astype(F32)
        for y in range(n_y):
            match_y[y * slots : (y + 1) * slots, lanes] = jnp.where(
                need_rows[:, y : y + 1] == have_wide, 1.0, 0.0
            ).astype(BF16)
        match_y[n_y * slots :, lanes] = jnp.where(own_rows == have[0:1], 1.0, 0.0).astype(BF16)

    def total(levels, scales):
        return jnp.sum(levels.astype(F32) * scales, axis=0)

    n_zneed, n_yneed = n_z * slots, n_y * slots
    x_total = jnp.zeros_like(x_own)
    y_first = y_own
    for it in range(ITERS):
        last = it + 1 == ITERS
        x_in()
        sums = jnp.dot(
            match_z[...],
            px_dst[it].reshape(n_x * 2 * slots, TILE),
            preferred_element_type=F32,
        )
        zq_src[it], zs_src[it] = quantize(sums[:n_zneed].reshape(n_z, slots, TILE))
        zq_in = send(z_peer, n_z - 1, lambda at: zq_src.at[it, at], zq_dst.at[it], my_z)
        zs_in = send(z_peer, n_z - 1, lambda at: zs_src.at[it, at], zs_dst.at[it], my_z)
        zo_src[it] = sums[n_zneed:].reshape(n_z, SHARE, TILE)
        zo_in = send(z_peer, n_z - 1, lambda at: zo_src.at[it, at], zo_dst.at[it], my_z)
        zq_dst[it, my_z] = zq_src[it, my_z]
        zs_dst[it, my_z] = zs_src[it, my_z]
        zo_dst[it, my_z] = zo_src[it, my_z]
        if it > 0:
            yo_in()
            y_first = project_dual(
                y_own + DUAL_STEP * (rhs_own - jnp.sum(yo_dst[...], axis=0)), rkind_own
            )
            mid_src[...] = y_first
            mid_in = send(y_peer, n_y - 1, lambda at: mid_src, mid_dst, my_y)
            mid_dst[my_y] = y_first
        zq_in()
        zs_in()
        x_new = project_primal(
            x_need - PRIMAL_STEP * (cost_need - total(zq_dst[it], zs_dst[it])),
            kind_need,
            upper_need,
        )
        put_split(pc_src.at[it], fore((2.0 * x_new - x_need).astype(BF16)))
        x_need = x_new
        c_in = send(core_peer, n_core - 1, lambda at: pc_src.at[it], pc_dst.at[it], my_core)
        pc_dst[it, my_core] = pc_src[it]
        zo_in()
        x_own = project_primal(
            x_own - PRIMAL_STEP * (cost_own - jnp.sum(zo_dst[it], axis=0)), kind_own, upper_own
        )
        x_total = x_total + x_own
        c_in()
        parts = pc_dst[it].reshape(n_core * 2 * slots, TILE)
        if not last:
            sums = jnp.dot(match_y[...], parts, preferred_element_type=F32)
            yq_src[...], ys_src[...] = quantize(sums[:n_yneed].reshape(n_y, slots, TILE))
            yq_in = send(y_peer, n_y - 1, lambda at: yq_src.at[at], yq_dst.at[it], my_y)
            ys_in = send(y_peer, n_y - 1, lambda at: ys_src.at[at], ys_dst.at[it], my_y)
            yo_src[...] = sums[n_yneed:].reshape(n_y, SHARE, TILE)
            yo_in = send(y_peer, n_y - 1, lambda at: yo_src.at[at], yo_dst, my_y)
            yq_dst[it, my_y] = yq_src[my_y]
            ys_dst[it, my_y] = ys_src[my_y]
            yo_dst[my_y] = yo_src[my_y]
            yq_in()
            ys_in()
            y_need = project_dual(
                y_need + DUAL_STEP * (rhs_need - total(yq_dst[it], ys_dst[it])), rkind_need
            )
            put_split(
                px_src.at[it + 1], back(y_need.astype(BF16).astype(F32), lambda g: None)
            )
            x_in = send(x_peer, n_x - 1, lambda at: px_src.at[it + 1], px_dst.at[it + 1], my_x)
            px_dst[it + 1, my_x] = px_src[it + 1]

    sums = jnp.dot(match_y[n_yneed:], parts, preferred_element_type=F32)
    lq_src[...], ls_src[...] = quantize(sums)
    yq_in = send(y_peer, n_y - 1, lambda at: lq_src, yq_dst.at[ITERS - 1], my_y)
    ys_in = send(y_peer, n_y - 1, lambda at: ls_src, ys_dst.at[ITERS - 1], my_y)
    primal_avg = x_total / ITERS
    po_src[...] = jnp.sum(cost_own * primal_avg, axis=0, keepdims=True)
    po_in = send(y_peer, n_y - 1, lambda at: po_src, po_dst, my_y)
    yq_dst[ITERS - 1, my_y] = lq_src[...]
    ys_dst[ITERS - 1, my_y] = ls_src[...]
    po_dst[my_y] = po_src[...]
    half_rhs = row_vecs[1].reshape(n_y, n_core, SHARE, TILE)
    half_kind = row_kind_full[...].reshape(n_y, n_core, SHARE, TILE)

    def of_core(both):
        one = both[:, 0]
        for k in range(1, n_core):
            one = jnp.where(my_core == k, both[:, k], one)
        return one.reshape(n_y * SHARE, TILE)

    half_rhs, half_kind = of_core(half_rhs), of_core(half_kind)
    mid_in()
    half_y = mid_dst[...].reshape(n_y * SHARE, TILE)
    po_in()
    fin_src[0:1] = jnp.sum(po_dst[...], axis=0)
    yq_in()
    ys_in()
    half_new = project_dual(
        half_y + DUAL_STEP * (half_rhs - total(yq_dst[ITERS - 1], ys_dst[ITERS - 1])), half_kind
    )
    half_avg = (half_y + half_new) / ITERS
    fin_src[1:2] = jnp.sum(half_rhs * half_avg, axis=0, keepdims=True)
    me_last = me_row * n_core + my_core
    fin_in = send(last_peer, n_last - 1, lambda at: fin_src, fin_dst, me_last)
    fin_dst[me_last] = fin_src[...]
    last_y[0] = half_new
    last_y[1] = half_avg
    mine = pl.ds(pl.multiple_of(my_y * SHARE, SHARE), SHARE)
    out_ref[0] = x_own
    out_ref[1] = last_y[0, mine]
    out_ref[2] = primal_avg
    out_ref[3] = last_y[1, mine]
    for both, which in pending[:-1]:
        pltpu.make_async_copy(both, both, send_sems.at[which]).wait()
    fin_in()
    inner = jnp.sum(jnp.sum(fin_dst[...], axis=0), axis=1, keepdims=True)
    primal_scale = 1.0 / math.sqrt(n_cblocks * TILE * n_col)
    dual_scale = 1.0 / math.sqrt(n_rblocks * TILE * n_row)
    first = lax.broadcasted_iota(I32, (SHARE, TILE), 1) == 0
    out_ref[4] = jnp.where(first, inner[0:1] * primal_scale, inner[1:2] * dual_scale)
    both, which = pending[-1]
    pltpu.make_async_copy(both, both, send_sems.at[which]).wait()


def split_kernel(packed_ref, *out_refs):
    for i in range(4):
        out_refs[i][...] = packed_ref[i]
    out_refs[4][...] = packed_ref[4, 0:1, 0:2]


def solution(mesh):
    n_row, n_col = mesh.shape["row"], mesh.shape["col"]
    n_x, n_core = N_X, N_CORE
    n_z, n_y = n_row // n_x, n_col // n_core

    def body(
        tiles,
        tile_rows,
        tile_cols,
        tile_count,
        cost,
        upper,
        var_kind,
        rhs,
        row_kind,
        primal_start,
        dual_start,
    ):
        slots = tiles.shape[2]
        sizes = (n_x, n_z, n_y, n_core, slots)
        n_rblocks, n_cblocks = n_col * SHARE, n_row * SHARE
        n_last = n_row * n_core
        anywhere = pl.BlockSpec(memory_space=pl.ANY)
        vmem = pl.BlockSpec(memory_space=pltpu.VMEM)
        smem = pl.BlockSpec(memory_space=pltpu.SMEM)
        scratch = [
            ((slots, TILE, TILE), BF16),
            ((2, 1, slots), I32),
            ((3, n_cblocks, TILE), F32),
            ((n_cblocks, TILE), I32),
            ((2, n_rblocks, TILE), F32),
            ((n_rblocks, TILE), I32),
            ((2, TILE), I32),
            ((n_x, 2, TILE), I32),
            ((n_z, 2, TILE), I32),
            ((n_y, 2, TILE), I32),
            ((n_core, 2, TILE), I32),
            ((n_z * (slots + SHARE), n_x * TILE), BF16),
            ((n_y * (slots + SHARE), n_core * TILE), BF16),
            ((ITERS, 2 * slots, TILE), BF16),
            ((ITERS, n_x, 2 * slots, TILE), BF16),
            ((ITERS, n_z, slots, TILE), I16),
            ((ITERS, n_z, slots, TILE), I16),
            ((ITERS, n_z, 1, TILE), F32),
            ((ITERS, n_z, 1, TILE), F32),
            ((ITERS, n_z, SHARE, TILE), F32),
            ((ITERS, n_z, SHARE, TILE), F32),
            ((ITERS, 2 * slots, TILE), BF16),
            ((ITERS, n_core, 2 * slots, TILE), BF16),
            ((n_y, slots, TILE), I16),
            ((ITERS, n_y, slots, TILE), I16),
            ((n_y, 1, TILE), F32),
            ((ITERS, n_y, 1, TILE), F32),
            ((n_y, SHARE, TILE), F32),
            ((n_y, SHARE, TILE), F32),
            ((n_y * SHARE, TILE), I16),
            ((1, TILE), F32),
            ((SHARE, TILE), F32),
            ((n_y, SHARE, TILE), F32),
            ((1, TILE), F32),
            ((n_y, 1, TILE), F32),
            ((2, n_y * SHARE, TILE), F32),
            ((2, TILE), F32),
            ((n_last, 2, TILE), F32),
        ]
        packed = pl.pallas_call(
            functools.partial(kernel, sizes),
            out_shape=jax.ShapeDtypeStruct((5, SHARE, TILE), F32),
            in_specs=[anywhere] * 3 + [smem] + [anywhere] * 7,
            out_specs=vmem,
            scratch_shapes=[pltpu.VMEM(shape, dtype) for shape, dtype in scratch]
            + [
                pltpu.SemaphoreType.DMA((9 + slots // GROUP,)),
                pltpu.SemaphoreType.DMA((SEMS,)),
                pltpu.SemaphoreType.DMA((SEMS,)),
            ],
            compiler_params=pltpu.CompilerParams(
                collective_id=0, has_side_effects=True, vmem_limit_bytes=60 * 2**20
            ),
            name="pdhg",
        )(
            tiles.reshape(slots, TILE, TILE),
            tile_rows.reshape(1, slots),
            tile_cols.reshape(1, slots),
            tile_count,
            cost.reshape(n_cblocks, TILE),
            upper.reshape(n_cblocks, TILE),
            var_kind.reshape(n_cblocks, TILE),
            rhs.reshape(n_rblocks, TILE),
            row_kind.reshape(n_rblocks, TILE),
            primal_start.reshape(n_cblocks, TILE),
            dual_start.reshape(n_rblocks, TILE),
        )
        share = jax.ShapeDtypeStruct((SHARE, TILE), F32)
        outs = pl.pallas_call(
            split_kernel,
            out_shape=(share,) * 4 + (jax.ShapeDtypeStruct((1, 2), F32),),
            in_specs=[vmem],
            out_specs=(vmem,) * 5,
            name="unpack",
        )(packed)
        return tuple(o.reshape(-1) for o in outs)

    placed = (
        P("row", "col", None, None, None),
        P("row", "col", None),
        P("row", "col", None),
        P("row", "col"),
        P("col"),
        P("col"),
        P("col"),
        P("row"),
        P("row"),
        P("col"),
        P("row"),
    )
    return jax.shard_map(
        body,
        mesh=mesh,
        in_specs=placed,
        out_specs=(P(("col", "row")), P(("row", "col")), P(("col", "row")), P(("row", "col")), P()),
        check_vma=False,
    )
```

```python
import functools
import math

import jax
import jax.numpy as jnp
from jax import lax
from jax.experimental import pallas as pl
from jax.experimental.pallas import tpu as pltpu
from jax.sharding import PartitionSpec as P

MESH = pl.DeviceIdType.MESH
TILE = 128
SHARE = 8
GROUP = 16
ITERS = 2
N_X = 4
N_CORE = 2
LEVELS = 32767.0
PRIMAL_STEP = 0.4
DUAL_STEP = 0.4
BF16 = jnp.bfloat16
F32 = jnp.float32
I32 = jnp.int32
I16 = jnp.int16
SEMS = 24


def project_primal(value, var_kind, upper):
    lower_cut = jnp.where(var_kind == 2, value, jnp.maximum(value, 0.0))
    return jnp.where(var_kind == 0, jnp.minimum(lower_cut, upper), lower_cut)


def project_dual(value, row_kind):
    return jnp.where(row_kind == 1, jnp.maximum(value, 0.0), value)


def zigzag(step, size):
    half = lax.div(step + 1, 2)
    return size // 2 + jnp.where(lax.rem(step, 2) == 0, half, -half)


def twice(row):
    wide = jnp.broadcast_to(row, (8, TILE))
    lane = lax.broadcasted_iota(I32, wide.shape, 1)
    return jnp.where(lane < TILE // 2, wide, pltpu.roll(wide, TILE // 2, 1))


def lane_top(sums):
    return jnp.max(jnp.abs(sums), axis=-2, keepdims=True)


def levels_of(sums, top):
    inverse = LEVELS / jnp.maximum(top, 1e-30)
    return jnp.round(sums * inverse).astype(I32).astype(I16)


def kernel(
    sizes,
    tiles_hbm,
    trow_hbm,
    tcol_hbm,
    count_ref,
    cost_hbm,
    upper_hbm,
    kind_hbm,
    rhs_hbm,
    rkind_hbm,
    primal_hbm,
    dual_hbm,
    out_ref,
    tiles,
    raw_idx,
    col_vecs,
    col_kind,
    row_vecs,
    row_kind_full,
    idx_src,
    idx_x,
    idx_z,
    idx_y,
    idx_c,
    match_z,
    match_y,
    px_src,
    px_dst,
    zq_src,
    zq_dst,
    zs_src,
    zs_dst,
    zo_src,
    zo_dst,
    pc_src,
    pc_dst,
    yq_src,
    yq_dst,
    ys_src,
    ys_dst,
    yo_src,
    yo_dst,
    lq_src,
    ls_src,
    mid_src,
    mid_dst,
    po_src,
    po_dst,
    last_y,
    fin_src,
    fin_dst,
    load_sems,
    send_sems,
    recv_sems,
):
    n_x, n_z, n_y, n_core, slots = sizes
    n_row, n_col = n_x * n_z, n_y * n_core
    n_rblocks, n_cblocks = n_col * SHARE, n_row * SHARE
    me_row = lax.axis_index("row")
    me_col = lax.axis_index("col")
    my_x, my_z = lax.div(me_row, n_z), lax.rem(me_row, n_z)
    my_y, my_core = lax.div(me_col, n_core), lax.rem(me_col, n_core)

    def x_peer(step):
        at = lax.rem(my_x + zigzag(step, n_x), n_x)
        return at, (at * n_z + my_z, me_col)

    def z_peer(step):
        at = lax.rem(my_z + zigzag(step, n_z), n_z)
        return at, (my_x * n_z + at, me_col)

    def y_peer(step):
        at = lax.rem(my_y + zigzag(step, n_y), n_y)
        return at, (me_row, at * n_core + my_core)

    def core_peer(step):
        at = lax.rem(my_core + 1 + step, n_core)
        return at, (me_row, my_y * n_core + at)

    def last_peer(step):
        ahead = lax.div(step, n_core)
        at_z = lax.rem(my_z + zigzag(lax.div(ahead, n_x), n_z), n_z)
        at_x = lax.rem(my_x + zigzag(lax.rem(ahead, n_x), n_x), n_x)
        at_core = lax.rem(my_core + n_core - 1 - lax.rem(step, n_core), n_core)
        return step, (at_x * n_z + at_z, my_y * n_core + at_core)

    n_last = n_row * n_core
    n_groups = slots // GROUP
    pieces = [pl.ds(g * GROUP, GROUP) for g in range(n_groups)]
    first_loads = [
        (trow_hbm, raw_idx.at[0]),
        (tcol_hbm, raw_idx.at[1]),
        (dual_hbm, row_vecs.at[0]),
    ]
    tile_loads = [(tiles_hbm.at[piece], tiles.at[piece]) for piece in pieces]
    late_loads = [
        (primal_hbm, col_vecs.at[0]),
        (cost_hbm, col_vecs.at[1]),
        (upper_hbm, col_vecs.at[2]),
        (kind_hbm, col_kind),
        (rhs_hbm, row_vecs.at[1]),
        (rkind_hbm, row_kind_full),
    ]
    copies = [
        pltpu.make_async_copy(src, dst, load_sems.at[i])
        for i, (src, dst) in enumerate(first_loads + tile_loads + late_loads)
    ]
    for copy in copies:
        copy.start()
    barrier = pltpu.get_barrier_semaphore()

    greeted = ((z_peer, n_z - 1), (y_peer, n_y - 1), (x_peer, n_x - 1), (core_peer, n_core - 1))
    for peer, count in greeted:

        @pl.loop(0, count)
        def _(step):
            pl.semaphore_signal(barrier, inc=1, device_id=peer(step)[1], device_id_type=MESH)

    n_first, n_tile = len(first_loads), len(tile_loads)
    for copy in copies[:n_first]:
        copy.wait()

    live = lax.broadcasted_iota(I32, (1, slots), 1) < count_ref[0, 0]
    block_rows = jnp.where(live, raw_idx[0], -1)
    block_cols = jnp.where(live, raw_idx[1], -1)
    row_pick = (
        (lax.broadcasted_iota(I32, (n_rblocks, slots), 0) == block_rows).astype(F32).T
    )
    sub = lax.broadcasted_iota(I32, (GROUP, TILE), 0)

    def back(part_of, ready):
        products = []
        for g in range(n_groups):
            ready(g)
            part = part_of[g * GROUP : (g + 1) * GROUP]
            spread = jnp.concatenate(
                [jnp.where(sub == j, part, 0.0).astype(BF16) for j in range(GROUP)], axis=1
            )
            block = tiles[g * GROUP : (g + 1) * GROUP].reshape(GROUP * TILE, TILE)
            products.append(jnp.dot(spread, block, preferred_element_type=F32))
        return jnp.concatenate(products, axis=0)

    def fore(part_of):
        products = []
        for g in range(n_groups):
            part = part_of[g * GROUP : (g + 1) * GROUP]
            block = tiles[g * GROUP : (g + 1) * GROUP].reshape(GROUP * TILE, TILE)
            every = lax.dot_general(
                part, block, (((1,), (1,)), ((), ())), preferred_element_type=F32
            )
            own = jnp.zeros((GROUP, TILE), F32)
            for j in range(GROUP):
                own = own + jnp.where(sub == j, every[:, j * TILE : (j + 1) * TILE], 0.0)
            products.append(own)
        return jnp.concatenate(products, axis=0)

    pending = []
    used = [0]

    def send(peer, count, source, dest, slot):
        sem = used[0]
        used[0] += 1

        @pl.loop(0, count)
        def _(step):
            at, device = peer(step)
            pltpu.make_async_remote_copy(
                src_ref=source(at),
                dst_ref=dest.at[slot],
                send_sem=send_sems.at[sem],
                recv_sem=recv_sems.at[sem],
                device_id=device,
                device_id_type=MESH,
            ).start()

        both = dest.at[pl.ds(0, count)]
        pending.append((both, sem))

        def arrive():
            pltpu.make_async_copy(both, both, recv_sems.at[sem]).wait()

        return arrive

    def put_split(ref, products):
        high = products.astype(BF16)
        ref[0:slots] = high
        ref[slots : 2 * slots] = (products - high.astype(F32)).astype(BF16)

    rounded = row_vecs[0].astype(BF16)
    picked = jnp.dot(row_pick.astype(BF16), rounded, preferred_element_type=F32)
    put_split(px_src.at[0], back(picked, lambda g: copies[n_first + g].wait()))
    idx_src[...] = jnp.full((2, TILE), -1, I32)
    idx_src[0:1, 0:slots] = block_cols
    idx_src[1:2, 0:slots] = block_rows
    pl.semaphore_wait(barrier, sum(count for _, count in greeted))

    z_idx_in = send(z_peer, n_z - 1, lambda at: idx_src, idx_z, my_z)
    x_idx_in = send(x_peer, n_x - 1, lambda at: idx_src, idx_x, my_x)
    x_in = send(x_peer, n_x - 1, lambda at: px_src.at[0], px_dst.at[0], my_x)
    y_idx_in = send(y_peer, n_y - 1, lambda at: idx_src, idx_y, my_y)
    c_idx_in = send(core_peer, n_core - 1, lambda at: idx_src, idx_c, my_core)
    for mine, ref in ((my_x, idx_x), (my_z, idx_z), (my_y, idx_y), (my_core, idx_c)):
        ref[mine] = idx_src[...]
    px_dst[0, my_x] = px_src[0]

    for copy in copies[n_first + n_tile :]:
        copy.wait()
    col_pick = (
        (lax.broadcasted_iota(I32, (n_cblocks, slots), 0) == block_cols).astype(F32).T
    )
    col_all = jnp.concatenate(
        [col_vecs[0], col_vecs[1], col_vecs[2], col_kind[...].astype(F32)], axis=1
    )
    col_got = jnp.dot(
        col_pick, col_all, precision=lax.Precision.HIGHEST, preferred_element_type=F32
    )
    x_need, cost_need, upper_need, kind_need = (
        col_got[:, i * TILE : (i + 1) * TILE] for i in range(4)
    )
    row_all = jnp.concatenate(
        [row_vecs[0], row_vecs[1], row_kind_full[...].astype(F32)], axis=1
    )
    row_got = jnp.dot(
        row_pick, row_all, precision=lax.Precision.HIGHEST, preferred_element_type=F32
    )
    y_need, rhs_need, rkind_need = (row_got[:, i * TILE : (i + 1) * TILE] for i in range(3))
    row_share = pl.ds(pl.multiple_of(me_row * SHARE, SHARE), SHARE)
    col_share = pl.ds(pl.multiple_of(me_col * SHARE, SHARE), SHARE)
    x_own, cost_own, upper_own = (col_vecs[i, row_share] for i in range(3))
    kind_own = col_kind[row_share]
    y_own, rhs_own, rkind_own = row_vecs[0, col_share], row_vecs[1, col_share], row_kind_full[col_share]

    z_idx_in()
    x_idx_in()
    need_cols = idx_z[:, 0, :].astype(F32).T[:slots]
    own_cols = lax.broadcasted_iota(I32, (n_z * SHARE, TILE), 0) + my_x * (n_z * SHARE)
    for k in range(n_x):
        have = twice(idx_x[k, 0:1])
        lanes = slice(k * TILE, (k + 1) * TILE)
        have_wide = jnp.broadcast_to(have[0:1], (slots, TILE)).astype(F32)
        for z in range(n_z):
            match_z[z * slots : (z + 1) * slots, lanes] = jnp.where(
                need_cols[:, z : z + 1] == have_wide, 1.0, 0.0
            ).astype(BF16)
        match_z[n_z * slots :, lanes] = jnp.where(own_cols == have[0:1], 1.0, 0.0).astype(BF16)
    y_idx_in()
    c_idx_in()
    need_rows = idx_y[:, 1, :].astype(F32).T[:slots]
    own_at = lax.broadcasted_iota(I32, (n_y * SHARE, TILE), 0)
    own_rows = (lax.div(own_at, SHARE) * n_core + my_core) * SHARE + lax.rem(own_at, SHARE)
    for k in range(n_core):
        have = twice(idx_c[k, 1:2])
        lanes = slice(k * TILE, (k + 1) * TILE)
        have_wide = jnp.broadcast_to(have[0:1], (slots, TILE)).astype(F32)
        for y in range(n_y):
            match_y[y * slots : (y + 1) * slots, lanes] = jnp.where(
                need_rows[:, y : y + 1] == have_wide, 1.0, 0.0
            ).astype(BF16)
        match_y[n_y * slots :, lanes] = jnp.where(own_rows == have[0:1], 1.0, 0.0).astype(BF16)

    def total(levels, scales):
        return jnp.sum(levels.astype(F32) * scales, axis=0)

    n_zneed, n_yneed = n_z * slots, n_y * slots
    x_total = jnp.zeros_like(x_own)
    y_first = y_own
    for it in range(ITERS):
        last = it + 1 == ITERS
        x_in()
        sums = jnp.dot(
            match_z[...],
            px_dst[it].reshape(n_x * 2 * slots, TILE),
            preferred_element_type=F32,
        )
        wanted = sums[:n_zneed].reshape(n_z, slots, TILE)
        top = lane_top(wanted)
        zs_src[it] = top * (1.0 / LEVELS)
        zs_in = send(z_peer, n_z - 1, lambda at: zs_src.at[it, at], zs_dst.at[it], my_z)
        zq_src[it] = levels_of(wanted, top)
        zq_in = send(z_peer, n_z - 1, lambda at: zq_src.at[it, at], zq_dst.at[it], my_z)
        zo_src[it] = sums[n_zneed:].reshape(n_z, SHARE, TILE)
        if last:
            zo_in = send(z_peer, n_z - 1, lambda at: zo_src.at[it, at], zo_dst.at[it], my_z)
        zq_dst[it, my_z] = zq_src[it, my_z]
        zs_dst[it, my_z] = zs_src[it, my_z]
        zo_dst[it, my_z] = zo_src[it, my_z]
        if it > 0:
            yo_in()
            y_first = project_dual(
                y_own + DUAL_STEP * (rhs_own - jnp.sum(yo_dst[...], axis=0)), rkind_own
            )
            mid_src[...] = y_first
            mid_in = send(y_peer, n_y - 1, lambda at: mid_src, mid_dst, my_y)
            mid_dst[my_y] = y_first
        zq_in()
        zs_in()
        x_new = project_primal(
            x_need - PRIMAL_STEP * (cost_need - total(zq_dst[it], zs_dst[it])),
            kind_need,
            upper_need,
        )
        if not last:
            zo_in = send(z_peer, n_z - 1, lambda at: zo_src.at[it, at], zo_dst.at[it], my_z)
        put_split(pc_src.at[it], fore((2.0 * x_new - x_need).astype(BF16)))
        x_need = x_new
        c_in = send(core_peer, n_core - 1, lambda at: pc_src.at[it], pc_dst.at[it], my_core)
        pc_dst[it, my_core] = pc_src[it]
        if last:
            zo_in()
            x_own = project_primal(
                x_own - PRIMAL_STEP * (cost_own - jnp.sum(zo_dst[it], axis=0)), kind_own, upper_own
            )
            x_total = x_total + x_own
        c_in()
        parts = pc_dst[it].reshape(n_core * 2 * slots, TILE)
        if not last:
            sums = jnp.dot(match_y[...], parts, preferred_element_type=F32)
            wanted = sums[:n_yneed].reshape(n_y, slots, TILE)
            top = lane_top(wanted)
            ys_src[...] = top * (1.0 / LEVELS)
            ys_in = send(y_peer, n_y - 1, lambda at: ys_src.at[at], ys_dst.at[it], my_y)
            yq_src[...] = levels_of(wanted, top)
            yq_in = send(y_peer, n_y - 1, lambda at: yq_src.at[at], yq_dst.at[it], my_y)
            yo_src[...] = sums[n_yneed:].reshape(n_y, SHARE, TILE)
            yq_dst[it, my_y] = yq_src[my_y]
            ys_dst[it, my_y] = ys_src[my_y]
            yo_dst[my_y] = yo_src[my_y]
            zo_in()
            x_own = project_primal(
                x_own - PRIMAL_STEP * (cost_own - jnp.sum(zo_dst[it], axis=0)), kind_own, upper_own
            )
            x_total = x_total + x_own
            yq_in()
            ys_in()
            yo_in = send(y_peer, n_y - 1, lambda at: yo_src.at[at], yo_dst, my_y)
            y_need = project_dual(
                y_need + DUAL_STEP * (rhs_need - total(yq_dst[it], ys_dst[it])), rkind_need
            )
            put_split(
                px_src.at[it + 1], back(y_need.astype(BF16).astype(F32), lambda g: None)
            )
            x_in = send(x_peer, n_x - 1, lambda at: px_src.at[it + 1], px_dst.at[it + 1], my_x)
            px_dst[it + 1, my_x] = px_src[it + 1]

    sums = jnp.dot(match_y[n_yneed:], parts, preferred_element_type=F32)
    top = lane_top(sums)
    ls_src[...] = top * (1.0 / LEVELS)
    ys_in = send(y_peer, n_y - 1, lambda at: ls_src, ys_dst.at[ITERS - 1], my_y)
    lq_src[...] = levels_of(sums, top)
    yq_in = send(y_peer, n_y - 1, lambda at: lq_src, yq_dst.at[ITERS - 1], my_y)
    primal_avg = x_total / ITERS
    po_src[...] = jnp.sum(cost_own * primal_avg, axis=0, keepdims=True)
    po_in = send(y_peer, n_y - 1, lambda at: po_src, po_dst, my_y)
    yq_dst[ITERS - 1, my_y] = lq_src[...]
    ys_dst[ITERS - 1, my_y] = ls_src[...]
    po_dst[my_y] = po_src[...]
    half_rhs = row_vecs[1].reshape(n_y, n_core, SHARE, TILE)
    half_kind = row_kind_full[...].reshape(n_y, n_core, SHARE, TILE)

    def of_core(both):
        one = both[:, 0]
        for k in range(1, n_core):
            one = jnp.where(my_core == k, both[:, k], one)
        return one.reshape(n_y * SHARE, TILE)

    half_rhs, half_kind = of_core(half_rhs), of_core(half_kind)
    mid_in()
    half_y = mid_dst[...].reshape(n_y * SHARE, TILE)
    po_in()
    fin_src[0:1] = jnp.sum(po_dst[...], axis=0)
    yq_in()
    ys_in()
    half_new = project_dual(
        half_y + DUAL_STEP * (half_rhs - total(yq_dst[ITERS - 1], ys_dst[ITERS - 1])), half_kind
    )
    half_avg = (half_y + half_new) / ITERS
    fin_src[1:2] = jnp.sum(half_rhs * half_avg, axis=0, keepdims=True)
    me_last = me_row * n_core + my_core
    fin_in = send(last_peer, n_last - 1, lambda at: fin_src, fin_dst, me_last)
    fin_dst[me_last] = fin_src[...]
    last_y[0] = half_new
    last_y[1] = half_avg
    mine = pl.ds(pl.multiple_of(my_y * SHARE, SHARE), SHARE)
    out_ref[0] = x_own
    out_ref[1] = last_y[0, mine]
    out_ref[2] = primal_avg
    out_ref[3] = last_y[1, mine]
    for both, which in pending[:-1]:
        pltpu.make_async_copy(both, both, send_sems.at[which]).wait()
    fin_in()
    inner = jnp.sum(jnp.sum(fin_dst[...], axis=0), axis=1, keepdims=True)
    primal_scale = 1.0 / math.sqrt(n_cblocks * TILE * n_col)
    dual_scale = 1.0 / math.sqrt(n_rblocks * TILE * n_row)
    first = lax.broadcasted_iota(I32, (SHARE, TILE), 1) == 0
    out_ref[4] = jnp.where(first, inner[0:1] * primal_scale, inner[1:2] * dual_scale)
    both, which = pending[-1]
    pltpu.make_async_copy(both, both, send_sems.at[which]).wait()


def split_kernel(packed_ref, *out_refs):
    for i in range(4):
        out_refs[i][...] = packed_ref[i]
    out_refs[4][...] = packed_ref[4, 0:1, 0:2]


def solution(mesh):
    n_row, n_col = mesh.shape["row"], mesh.shape["col"]
    n_x, n_core = N_X, N_CORE
    n_z, n_y = n_row // n_x, n_col // n_core

    def body(
        tiles,
        tile_rows,
        tile_cols,
        tile_count,
        cost,
        upper,
        var_kind,
        rhs,
        row_kind,
        primal_start,
        dual_start,
    ):
        slots = tiles.shape[2]
        sizes = (n_x, n_z, n_y, n_core, slots)
        n_rblocks, n_cblocks = n_col * SHARE, n_row * SHARE
        n_last = n_row * n_core
        anywhere = pl.BlockSpec(memory_space=pl.ANY)
        vmem = pl.BlockSpec(memory_space=pltpu.VMEM)
        smem = pl.BlockSpec(memory_space=pltpu.SMEM)
        scratch = [
            ((slots, TILE, TILE), BF16),
            ((2, 1, slots), I32),
            ((3, n_cblocks, TILE), F32),
            ((n_cblocks, TILE), I32),
            ((2, n_rblocks, TILE), F32),
            ((n_rblocks, TILE), I32),
            ((2, TILE), I32),
            ((n_x, 2, TILE), I32),
            ((n_z, 2, TILE), I32),
            ((n_y, 2, TILE), I32),
            ((n_core, 2, TILE), I32),
            ((n_z * (slots + SHARE), n_x * TILE), BF16),
            ((n_y * (slots + SHARE), n_core * TILE), BF16),
            ((ITERS, 2 * slots, TILE), BF16),
            ((ITERS, n_x, 2 * slots, TILE), BF16),
            ((ITERS, n_z, slots, TILE), I16),
            ((ITERS, n_z, slots, TILE), I16),
            ((ITERS, n_z, 1, TILE), F32),
            ((ITERS, n_z, 1, TILE), F32),
            ((ITERS, n_z, SHARE, TILE), F32),
            ((ITERS, n_z, SHARE, TILE), F32),
            ((ITERS, 2 * slots, TILE), BF16),
            ((ITERS, n_core, 2 * slots, TILE), BF16),
            ((n_y, slots, TILE), I16),
            ((ITERS, n_y, slots, TILE), I16),
            ((n_y, 1, TILE), F32),
            ((ITERS, n_y, 1, TILE), F32),
            ((n_y, SHARE, TILE), F32),
            ((n_y, SHARE, TILE), F32),
            ((n_y * SHARE, TILE), I16),
            ((1, TILE), F32),
            ((SHARE, TILE), F32),
            ((n_y, SHARE, TILE), F32),
            ((1, TILE), F32),
            ((n_y, 1, TILE), F32),
            ((2, n_y * SHARE, TILE), F32),
            ((2, TILE), F32),
            ((n_last, 2, TILE), F32),
        ]
        packed = pl.pallas_call(
            functools.partial(kernel, sizes),
            out_shape=jax.ShapeDtypeStruct((5, SHARE, TILE), F32),
            in_specs=[anywhere] * 3 + [smem] + [anywhere] * 7,
            out_specs=vmem,
            scratch_shapes=[pltpu.VMEM(shape, dtype) for shape, dtype in scratch]
            + [
                pltpu.SemaphoreType.DMA((9 + slots // GROUP,)),
                pltpu.SemaphoreType.DMA((SEMS,)),
                pltpu.SemaphoreType.DMA((SEMS,)),
            ],
            compiler_params=pltpu.CompilerParams(
                collective_id=0, has_side_effects=True, vmem_limit_bytes=60 * 2**20
            ),
            name="pdhg",
        )(
            tiles.reshape(slots, TILE, TILE),
            tile_rows.reshape(1, slots),
            tile_cols.reshape(1, slots),
            tile_count,
            cost.reshape(n_cblocks, TILE),
            upper.reshape(n_cblocks, TILE),
            var_kind.reshape(n_cblocks, TILE),
            rhs.reshape(n_rblocks, TILE),
            row_kind.reshape(n_rblocks, TILE),
            primal_start.reshape(n_cblocks, TILE),
            dual_start.reshape(n_rblocks, TILE),
        )
        share = jax.ShapeDtypeStruct((SHARE, TILE), F32)
        outs = pl.pallas_call(
            split_kernel,
            out_shape=(share,) * 4 + (jax.ShapeDtypeStruct((1, 2), F32),),
            in_specs=[vmem],
            out_specs=(vmem,) * 5,
            name="unpack",
        )(packed)
        return tuple(o.reshape(-1) for o in outs)

    placed = (
        P("row", "col", None, None, None),
        P("row", "col", None),
        P("row", "col", None),
        P("row", "col"),
        P("col"),
        P("col"),
        P("col"),
        P("row"),
        P("row"),
        P("col"),
        P("row"),
    )
    return jax.shard_map(
        body,
        mesh=mesh,
        in_specs=placed,
        out_specs=(P(("col", "row")), P(("row", "col")), P(("col", "row")), P(("row", "col")), P()),
        check_vma=False,
    )
```

```python
import functools
import math

import jax
import jax.numpy as jnp
from jax import lax
from jax.experimental import pallas as pl
from jax.experimental.pallas import tpu as pltpu
from jax.sharding import PartitionSpec as P

MESH = pl.DeviceIdType.MESH
TILE = 128
SHARE = 8
GROUP = 16
ITERS = 2
N_X = 4
N_CORE = 2
LEVELS = 32767.0
PRIMAL_STEP = 0.4
DUAL_STEP = 0.4
BF16 = jnp.bfloat16
F32 = jnp.float32
I32 = jnp.int32
I16 = jnp.int16
SEMS = 24


def project_primal(value, var_kind, upper):
    lower_cut = jnp.where(var_kind == 2, value, jnp.maximum(value, 0.0))
    return jnp.where(var_kind == 0, jnp.minimum(lower_cut, upper), lower_cut)


def project_dual(value, row_kind):
    return jnp.where(row_kind == 1, jnp.maximum(value, 0.0), value)


def zigzag(step, size):
    half = lax.div(step + 1, 2)
    return size // 2 + jnp.where(lax.rem(step, 2) == 0, half, -half)


def twice(row):
    wide = jnp.broadcast_to(row, (8, TILE))
    lane = lax.broadcasted_iota(I32, wide.shape, 1)
    return jnp.where(lane < TILE // 2, wide, pltpu.roll(wide, TILE // 2, 1))


def lane_top(sums):
    return jnp.max(jnp.abs(sums), axis=-2, keepdims=True)


def levels_of(sums, top):
    inverse = LEVELS / jnp.maximum(top, 1e-30)
    return jnp.round(sums * inverse).astype(I32).astype(I16)


def kernel(
    sizes,
    tiles_hbm,
    trow_hbm,
    tcol_hbm,
    count_ref,
    cost_hbm,
    upper_hbm,
    kind_hbm,
    rhs_hbm,
    rkind_hbm,
    primal_hbm,
    dual_hbm,
    out_ref,
    tiles,
    turned,
    raw_idx,
    col_vecs,
    col_kind,
    row_vecs,
    row_kind_full,
    idx_src,
    idx_x,
    idx_z,
    idx_y,
    idx_c,
    match_z,
    match_y,
    px_src,
    px_dst,
    zq_src,
    zq_dst,
    zs_src,
    zs_dst,
    zo_src,
    zo_dst,
    pc_src,
    pc_dst,
    yq_src,
    yq_dst,
    ys_src,
    ys_dst,
    yo_src,
    yo_dst,
    lq_src,
    ls_src,
    mid_src,
    mid_dst,
    po_src,
    po_dst,
    last_y,
    fin_src,
    fin_dst,
    load_sems,
    send_sems,
    recv_sems,
):
    n_x, n_z, n_y, n_core, slots = sizes
    n_row, n_col = n_x * n_z, n_y * n_core
    n_rblocks, n_cblocks = n_col * SHARE, n_row * SHARE
    me_row = lax.axis_index("row")
    me_col = lax.axis_index("col")
    my_x, my_z = lax.div(me_row, n_z), lax.rem(me_row, n_z)
    my_y, my_core = lax.div(me_col, n_core), lax.rem(me_col, n_core)

    def x_peer(step):
        at = lax.rem(my_x + zigzag(step, n_x), n_x)
        return at, (at * n_z + my_z, me_col)

    def z_peer(step):
        at = lax.rem(my_z + zigzag(step, n_z), n_z)
        return at, (my_x * n_z + at, me_col)

    def y_peer(step):
        at = lax.rem(my_y + zigzag(step, n_y), n_y)
        return at, (me_row, at * n_core + my_core)

    def core_peer(step):
        at = lax.rem(my_core + 1 + step, n_core)
        return at, (me_row, my_y * n_core + at)

    def last_peer(step):
        ahead = lax.div(step, n_core)
        at_z = lax.rem(my_z + zigzag(lax.div(ahead, n_x), n_z), n_z)
        at_x = lax.rem(my_x + zigzag(lax.rem(ahead, n_x), n_x), n_x)
        at_core = lax.rem(my_core + n_core - 1 - lax.rem(step, n_core), n_core)
        return step, (at_x * n_z + at_z, my_y * n_core + at_core)

    n_last = n_row * n_core
    n_groups = slots // GROUP
    pieces = [pl.ds(g * GROUP, GROUP) for g in range(n_groups)]
    first_loads = [
        (trow_hbm, raw_idx.at[0]),
        (tcol_hbm, raw_idx.at[1]),
        (dual_hbm, row_vecs.at[0]),
    ]
    tile_loads = [(tiles_hbm.at[piece], tiles.at[piece]) for piece in pieces]
    late_loads = [
        (primal_hbm, col_vecs.at[0]),
        (cost_hbm, col_vecs.at[1]),
        (upper_hbm, col_vecs.at[2]),
        (kind_hbm, col_kind),
        (rhs_hbm, row_vecs.at[1]),
        (rkind_hbm, row_kind_full),
    ]
    copies = [
        pltpu.make_async_copy(src, dst, load_sems.at[i])
        for i, (src, dst) in enumerate(first_loads + tile_loads + late_loads)
    ]
    for copy in copies:
        copy.start()
    barrier = pltpu.get_barrier_semaphore()

    greeted = ((z_peer, n_z - 1), (y_peer, n_y - 1), (x_peer, n_x - 1), (core_peer, n_core - 1))
    for peer, count in greeted:

        @pl.loop(0, count)
        def _(step):
            pl.semaphore_signal(barrier, inc=1, device_id=peer(step)[1], device_id_type=MESH)

    n_first, n_tile = len(first_loads), len(tile_loads)
    for copy in copies[:n_first]:
        copy.wait()

    live = lax.broadcasted_iota(I32, (1, slots), 1) < count_ref[0, 0]
    block_rows = jnp.where(live, raw_idx[0], -1)
    block_cols = jnp.where(live, raw_idx[1], -1)
    row_pick = (
        (lax.broadcasted_iota(I32, (n_rblocks, slots), 0) == block_rows).astype(F32).T
    )
    sub = lax.broadcasted_iota(I32, (GROUP, TILE), 0)

    def spread(part):
        return jnp.concatenate(
            [jnp.where(sub == j, part, 0.0).astype(BF16) for j in range(GROUP)], axis=1
        )

    def back(part_of, ready):
        products = []
        for g in range(n_groups):
            ready(g)
            part = part_of[g * GROUP : (g + 1) * GROUP]
            block = tiles[g * GROUP : (g + 1) * GROUP].reshape(GROUP * TILE, TILE)
            products.append(jnp.dot(spread(part), block, preferred_element_type=F32))
        return jnp.concatenate(products, axis=0)

    def fore(part_of):
        products = []
        for g in range(n_groups):
            part = part_of[g * GROUP : (g + 1) * GROUP]
            block = turned[g * GROUP : (g + 1) * GROUP].reshape(GROUP * TILE, TILE)
            products.append(jnp.dot(spread(part), block, preferred_element_type=F32))
        return jnp.concatenate(products, axis=0)

    pending = []
    used = [0]

    def send(peer, count, slot, *pairs):
        base = used[0]
        used[0] += len(pairs)

        @pl.loop(0, count)
        def _(step):
            at, device = peer(step)
            for k, (source, dest) in enumerate(pairs):
                pltpu.make_async_remote_copy(
                    src_ref=source(at),
                    dst_ref=dest.at[slot],
                    send_sem=send_sems.at[base + k],
                    recv_sem=recv_sems.at[base + k],
                    device_id=device,
                    device_id_type=MESH,
                ).start()

        started = [(dest.at[pl.ds(0, count)], base + k) for k, (_, dest) in enumerate(pairs)]
        pending.extend(started)

        def arrive():
            for both, sem in started:
                pltpu.make_async_copy(both, both, recv_sems.at[sem]).wait()

        return arrive

    def put_split(ref, products):
        high = products.astype(BF16)
        ref[0:slots] = high
        ref[slots : 2 * slots] = (products - high.astype(F32)).astype(BF16)

    rounded = row_vecs[0].astype(BF16)
    picked = jnp.dot(row_pick.astype(BF16), rounded, preferred_element_type=F32)
    put_split(px_src.at[0], back(picked, lambda g: copies[n_first + g].wait()))
    idx_src[...] = jnp.full((2, TILE), -1, I32)
    idx_src[0:1, 0:slots] = block_cols
    idx_src[1:2, 0:slots] = block_rows
    pl.semaphore_wait(barrier, sum(count for _, count in greeted))

    z_idx_in = send(z_peer, n_z - 1, my_z, (lambda at: idx_src, idx_z))
    x_idx_in = send(x_peer, n_x - 1, my_x, (lambda at: idx_src, idx_x))
    x_in = send(x_peer, n_x - 1, my_x, (lambda at: px_src.at[0], px_dst.at[0]))
    y_idx_in = send(y_peer, n_y - 1, my_y, (lambda at: idx_src, idx_y))
    c_idx_in = send(core_peer, n_core - 1, my_core, (lambda at: idx_src, idx_c))
    for mine, ref in ((my_x, idx_x), (my_z, idx_z), (my_y, idx_y), (my_core, idx_c)):
        ref[mine] = idx_src[...]
    px_dst[0, my_x] = px_src[0]

    for copy in copies[n_first + n_tile :]:
        copy.wait()
    col_pick = (
        (lax.broadcasted_iota(I32, (n_cblocks, slots), 0) == block_cols).astype(F32).T
    )
    col_all = jnp.concatenate(
        [col_vecs[0], col_vecs[1], col_vecs[2], col_kind[...].astype(F32)], axis=1
    )
    col_got = jnp.dot(
        col_pick, col_all, precision=lax.Precision.HIGHEST, preferred_element_type=F32
    )
    x_need, cost_need, upper_need, kind_need = (
        col_got[:, i * TILE : (i + 1) * TILE] for i in range(4)
    )
    row_share = pl.ds(pl.multiple_of(me_row * SHARE, SHARE), SHARE)
    col_share = pl.ds(pl.multiple_of(me_col * SHARE, SHARE), SHARE)
    x_own, cost_own, upper_own = (col_vecs[i, row_share] for i in range(3))
    kind_own = col_kind[row_share]
    y_own, rhs_own, rkind_own = row_vecs[0, col_share], row_vecs[1, col_share], row_kind_full[col_share]

    z_idx_in()
    x_idx_in()
    need_cols = idx_z[:, 0, :].astype(F32).T[:slots]
    own_cols = lax.broadcasted_iota(I32, (n_z * SHARE, TILE), 0) + my_x * (n_z * SHARE)
    for k in range(n_x):
        have = twice(idx_x[k, 0:1])
        lanes = slice(k * TILE, (k + 1) * TILE)
        have_wide = jnp.broadcast_to(have[0:1], (slots, TILE)).astype(F32)
        for z in range(n_z):
            match_z[z * slots : (z + 1) * slots, lanes] = jnp.where(
                need_cols[:, z : z + 1] == have_wide, 1.0, 0.0
            ).astype(BF16)
        match_z[n_z * slots :, lanes] = jnp.where(own_cols == have[0:1], 1.0, 0.0).astype(BF16)
    def total(levels, scales):
        return jnp.sum(levels.astype(F32) * scales, axis=0)

    n_zneed, n_yneed = n_z * slots, n_y * slots
    x_total = jnp.zeros_like(x_own)
    y_first = y_own
    for it in range(ITERS):
        last = it + 1 == ITERS
        x_in()
        sums = jnp.dot(
            match_z[...],
            px_dst[it].reshape(n_x * 2 * slots, TILE),
            preferred_element_type=F32,
        )
        wanted = sums[:n_zneed].reshape(n_z, slots, TILE)
        top = lane_top(wanted)
        zs_src[it] = top * (1.0 / LEVELS)
        zq_src[it] = levels_of(wanted, top)
        zq_in = send(
            z_peer,
            n_z - 1,
            my_z,
            (lambda at: zs_src.at[it, at], zs_dst.at[it]),
            (lambda at: zq_src.at[it, at], zq_dst.at[it]),
        )
        zo_src[it] = sums[n_zneed:].reshape(n_z, SHARE, TILE)
        if last:
            zo_in = send(z_peer, n_z - 1, my_z, (lambda at: zo_src.at[it, at], zo_dst.at[it]))
        zq_dst[it, my_z] = zq_src[it, my_z]
        zs_dst[it, my_z] = zs_src[it, my_z]
        zo_dst[it, my_z] = zo_src[it, my_z]
        if it > 0:
            yo_in()
            y_first = project_dual(
                y_own + DUAL_STEP * (rhs_own - jnp.sum(yo_dst[...], axis=0)), rkind_own
            )
            mid_src[...] = y_first
            mid_in = send(y_peer, n_y - 1, my_y, (lambda at: mid_src, mid_dst))
            mid_dst[my_y] = y_first
        if it == 0:
            row_all = jnp.concatenate(
                [row_vecs[0], row_vecs[1], row_kind_full[...].astype(F32)], axis=1
            )
            row_got = jnp.dot(
                row_pick, row_all, precision=lax.Precision.HIGHEST, preferred_element_type=F32
            )
            y_need, rhs_need, rkind_need = (row_got[:, i * TILE : (i + 1) * TILE] for i in range(3))
            y_idx_in()
            c_idx_in()
            need_rows = idx_y[:, 1, :].astype(F32).T[:slots]
            own_at = lax.broadcasted_iota(I32, (n_y * SHARE, TILE), 0)
            own_rows = (lax.div(own_at, SHARE) * n_core + my_core) * SHARE + lax.rem(own_at, SHARE)
            for k in range(n_core):
                have = twice(idx_c[k, 1:2])
                lanes = slice(k * TILE, (k + 1) * TILE)
                have_wide = jnp.broadcast_to(have[0:1], (slots, TILE)).astype(F32)
                for y in range(n_y):
                    match_y[y * slots : (y + 1) * slots, lanes] = jnp.where(
                        need_rows[:, y : y + 1] == have_wide, 1.0, 0.0
                    ).astype(BF16)
                match_y[n_y * slots :, lanes] = jnp.where(own_rows == have[0:1], 1.0, 0.0).astype(BF16)

            @pl.loop(0, slots // 8)
            def _(part):
                for k in range(8):
                    turned[part * 8 + k] = tiles[part * 8 + k].T

        zq_in()
        x_new = project_primal(
            x_need - PRIMAL_STEP * (cost_need - total(zq_dst[it], zs_dst[it])),
            kind_need,
            upper_need,
        )
        if not last:
            zo_in = send(z_peer, n_z - 1, my_z, (lambda at: zo_src.at[it, at], zo_dst.at[it]))
        put_split(pc_src.at[it], fore((2.0 * x_new - x_need).astype(BF16).astype(F32)))
        x_need = x_new
        c_in = send(core_peer, n_core - 1, my_core, (lambda at: pc_src.at[it], pc_dst.at[it]))
        pc_dst[it, my_core] = pc_src[it]
        if last:
            zo_in()
            x_own = project_primal(
                x_own - PRIMAL_STEP * (cost_own - jnp.sum(zo_dst[it], axis=0)), kind_own, upper_own
            )
            x_total = x_total + x_own
        c_in()
        parts = pc_dst[it].reshape(n_core * 2 * slots, TILE)
        if not last:
            sums = jnp.dot(match_y[...], parts, preferred_element_type=F32)
            wanted = sums[:n_yneed].reshape(n_y, slots, TILE)
            top = lane_top(wanted)
            ys_src[...] = top * (1.0 / LEVELS)
            yq_src[...] = levels_of(wanted, top)
            yq_in = send(
                y_peer,
                n_y - 1,
                my_y,
                (lambda at: ys_src.at[at], ys_dst.at[it]),
                (lambda at: yq_src.at[at], yq_dst.at[it]),
            )
            yo_src[...] = sums[n_yneed:].reshape(n_y, SHARE, TILE)
            yq_dst[it, my_y] = yq_src[my_y]
            ys_dst[it, my_y] = ys_src[my_y]
            yo_dst[my_y] = yo_src[my_y]
            zo_in()
            x_own = project_primal(
                x_own - PRIMAL_STEP * (cost_own - jnp.sum(zo_dst[it], axis=0)), kind_own, upper_own
            )
            x_total = x_total + x_own
            yq_in()
            yo_in = send(y_peer, n_y - 1, my_y, (lambda at: yo_src.at[at], yo_dst))
            y_need = project_dual(
                y_need + DUAL_STEP * (rhs_need - total(yq_dst[it], ys_dst[it])), rkind_need
            )
            put_split(
                px_src.at[it + 1], back(y_need.astype(BF16).astype(F32), lambda g: None)
            )
            x_in = send(x_peer, n_x - 1, my_x, (lambda at: px_src.at[it + 1], px_dst.at[it + 1]))
            px_dst[it + 1, my_x] = px_src[it + 1]

    sums = jnp.dot(match_y[n_yneed:], parts, preferred_element_type=F32)
    top = lane_top(sums)
    ls_src[...] = top * (1.0 / LEVELS)
    lq_src[...] = levels_of(sums, top)
    yq_in = send(
        y_peer,
        n_y - 1,
        my_y,
        (lambda at: ls_src, ys_dst.at[ITERS - 1]),
        (lambda at: lq_src, yq_dst.at[ITERS - 1]),
    )
    primal_avg = x_total / ITERS
    po_src[...] = jnp.sum(cost_own * primal_avg, axis=0, keepdims=True)
    po_in = send(y_peer, n_y - 1, my_y, (lambda at: po_src, po_dst))
    yq_dst[ITERS - 1, my_y] = lq_src[...]
    ys_dst[ITERS - 1, my_y] = ls_src[...]
    po_dst[my_y] = po_src[...]
    half_rhs = row_vecs[1].reshape(n_y, n_core, SHARE, TILE)
    half_kind = row_kind_full[...].reshape(n_y, n_core, SHARE, TILE)

    def of_core(both):
        one = both[:, 0]
        for k in range(1, n_core):
            one = jnp.where(my_core == k, both[:, k], one)
        return one.reshape(n_y * SHARE, TILE)

    half_rhs, half_kind = of_core(half_rhs), of_core(half_kind)
    mid_in()
    half_y = mid_dst[...].reshape(n_y * SHARE, TILE)
    po_in()
    fin_src[0:1] = jnp.sum(po_dst[...], axis=0)
    yq_in()
    half_new = project_dual(
        half_y + DUAL_STEP * (half_rhs - total(yq_dst[ITERS - 1], ys_dst[ITERS - 1])), half_kind
    )
    half_avg = (half_y + half_new) / ITERS
    fin_src[1:2] = jnp.sum(half_rhs * half_avg, axis=0, keepdims=True)
    me_last = me_row * n_core + my_core
    fin_in = send(last_peer, n_last - 1, me_last, (lambda at: fin_src, fin_dst))
    fin_dst[me_last] = fin_src[...]
    last_y[0] = half_new
    last_y[1] = half_avg
    mine = pl.ds(pl.multiple_of(my_y * SHARE, SHARE), SHARE)
    out_ref[0] = x_own
    out_ref[1] = last_y[0, mine]
    out_ref[2] = primal_avg
    out_ref[3] = last_y[1, mine]
    for both, which in pending[:-1]:
        pltpu.make_async_copy(both, both, send_sems.at[which]).wait()
    fin_in()
    inner = jnp.sum(jnp.sum(fin_dst[...], axis=0), axis=1, keepdims=True)
    primal_scale = 1.0 / math.sqrt(n_cblocks * TILE * n_col)
    dual_scale = 1.0 / math.sqrt(n_rblocks * TILE * n_row)
    first = lax.broadcasted_iota(I32, (SHARE, TILE), 1) == 0
    out_ref[4] = jnp.where(first, inner[0:1] * primal_scale, inner[1:2] * dual_scale)
    both, which = pending[-1]
    pltpu.make_async_copy(both, both, send_sems.at[which]).wait()


def split_kernel(packed_ref, *out_refs):
    for i in range(4):
        out_refs[i][...] = packed_ref[i]
    out_refs[4][...] = packed_ref[4, 0:1, 0:2]


def solution(mesh):
    n_row, n_col = mesh.shape["row"], mesh.shape["col"]
    n_x, n_core = N_X, N_CORE
    n_z, n_y = n_row // n_x, n_col // n_core

    def body(
        tiles,
        tile_rows,
        tile_cols,
        tile_count,
        cost,
        upper,
        var_kind,
        rhs,
        row_kind,
        primal_start,
        dual_start,
    ):
        slots = tiles.shape[2]
        sizes = (n_x, n_z, n_y, n_core, slots)
        n_rblocks, n_cblocks = n_col * SHARE, n_row * SHARE
        n_last = n_row * n_core
        anywhere = pl.BlockSpec(memory_space=pl.ANY)
        vmem = pl.BlockSpec(memory_space=pltpu.VMEM)
        smem = pl.BlockSpec(memory_space=pltpu.SMEM)
        scratch = [
            ((slots, TILE, TILE), BF16),
            ((slots, TILE, TILE), BF16),
            ((2, 1, slots), I32),
            ((3, n_cblocks, TILE), F32),
            ((n_cblocks, TILE), I32),
            ((2, n_rblocks, TILE), F32),
            ((n_rblocks, TILE), I32),
            ((2, TILE), I32),
            ((n_x, 2, TILE), I32),
            ((n_z, 2, TILE), I32),
            ((n_y, 2, TILE), I32),
            ((n_core, 2, TILE), I32),
            ((n_z * (slots + SHARE), n_x * TILE), BF16),
            ((n_y * (slots + SHARE), n_core * TILE), BF16),
            ((ITERS, 2 * slots, TILE), BF16),
            ((ITERS, n_x, 2 * slots, TILE), BF16),
            ((ITERS, n_z, slots, TILE), I16),
            ((ITERS, n_z, slots, TILE), I16),
            ((ITERS, n_z, 1, TILE), F32),
            ((ITERS, n_z, 1, TILE), F32),
            ((ITERS, n_z, SHARE, TILE), F32),
            ((ITERS, n_z, SHARE, TILE), F32),
            ((ITERS, 2 * slots, TILE), BF16),
            ((ITERS, n_core, 2 * slots, TILE), BF16),
            ((n_y, slots, TILE), I16),
            ((ITERS, n_y, slots, TILE), I16),
            ((n_y, 1, TILE), F32),
            ((ITERS, n_y, 1, TILE), F32),
            ((n_y, SHARE, TILE), F32),
            ((n_y, SHARE, TILE), F32),
            ((n_y * SHARE, TILE), I16),
            ((1, TILE), F32),
            ((SHARE, TILE), F32),
            ((n_y, SHARE, TILE), F32),
            ((1, TILE), F32),
            ((n_y, 1, TILE), F32),
            ((2, n_y * SHARE, TILE), F32),
            ((2, TILE), F32),
            ((n_last, 2, TILE), F32),
        ]
        def in_hbm(array):
            return pltpu.with_memory_space_constraint(array, pltpu.HBM)

        packed = pl.pallas_call(
            functools.partial(kernel, sizes),
            out_shape=pltpu.VMEM((5, SHARE, TILE), F32),
            in_specs=[anywhere] * 3 + [smem] + [anywhere] * 7,
            out_specs=vmem,
            scratch_shapes=[pltpu.VMEM(shape, dtype) for shape, dtype in scratch]
            + [
                pltpu.SemaphoreType.DMA((9 + slots // GROUP,)),
                pltpu.SemaphoreType.DMA((SEMS,)),
                pltpu.SemaphoreType.DMA((SEMS,)),
            ],
            compiler_params=pltpu.CompilerParams(
                collective_id=0, has_side_effects=True, vmem_limit_bytes=48 * 2**20
            ),
            name="pdhg",
        )(
            in_hbm(tiles.reshape(slots, TILE, TILE)),
            in_hbm(tile_rows.reshape(1, slots)),
            in_hbm(tile_cols.reshape(1, slots)),
            tile_count,
            in_hbm(cost.reshape(n_cblocks, TILE)),
            in_hbm(upper.reshape(n_cblocks, TILE)),
            in_hbm(var_kind.reshape(n_cblocks, TILE)),
            in_hbm(rhs.reshape(n_rblocks, TILE)),
            in_hbm(row_kind.reshape(n_rblocks, TILE)),
            in_hbm(primal_start.reshape(n_cblocks, TILE)),
            in_hbm(dual_start.reshape(n_rblocks, TILE)),
        )
        share = jax.ShapeDtypeStruct((SHARE, TILE), F32)
        outs = pl.pallas_call(
            split_kernel,
            out_shape=(share,) * 4 + (jax.ShapeDtypeStruct((1, 2), F32),),
            in_specs=[vmem],
            out_specs=(vmem,) * 5,
            name="unpack",
        )(pltpu.with_memory_space_constraint(packed, pltpu.VMEM))
        return tuple(o.reshape(-1) for o in outs)

    placed = (
        P("row", "col", None, None, None),
        P("row", "col", None),
        P("row", "col", None),
        P("row", "col"),
        P("col"),
        P("col"),
        P("col"),
        P("row"),
        P("row"),
        P("col"),
        P("row"),
    )
    return jax.shard_map(
        body,
        mesh=mesh,
        in_specs=placed,
        out_specs=(P(("col", "row")), P(("row", "col")), P(("col", "row")), P(("row", "col")), P()),
        check_vma=False,
    )
```

```python
import functools
import math

import jax
import jax.numpy as jnp
from jax import lax
from jax.experimental import pallas as pl
from jax.experimental.pallas import tpu as pltpu
from jax.sharding import PartitionSpec as P

MESH = pl.DeviceIdType.MESH
TILE = 128
SHARE = 8
GROUP = 16
ITERS = 2
N_X = 4
N_CORE = 2
LEVELS = 32767.0
PRIMAL_STEP = 0.4
DUAL_STEP = 0.4
BF16 = jnp.bfloat16
F32 = jnp.float32
I32 = jnp.int32
I16 = jnp.int16
SEMS = 24
CHUNKS = 2


def project_primal(value, var_kind, upper):
    lower_cut = jnp.where(var_kind == 2, value, jnp.maximum(value, 0.0))
    return jnp.where(var_kind == 0, jnp.minimum(lower_cut, upper), lower_cut)


def project_dual(value, row_kind):
    return jnp.where(row_kind == 1, jnp.maximum(value, 0.0), value)


def zigzag(step, size):
    if isinstance(step, int):
        return size // 2 + (step + 1) // 2 * (1 - 2 * (step % 2))
    half = lax.div(step + 1, 2)
    return size // 2 + jnp.where(lax.rem(step, 2) == 0, half, -half)


def backward(size):
    ahead = [zigzag(step, size) % size for step in range(size)]
    return [ahead.index((size - offset) % size) for offset in ahead]


def twice(row):
    wide = jnp.broadcast_to(row, (8, TILE))
    lane = lax.broadcasted_iota(I32, wide.shape, 1)
    return jnp.where(lane < TILE // 2, wide, pltpu.roll(wide, TILE // 2, 1))


def lane_top(sums):
    return jnp.max(jnp.abs(sums), axis=-2, keepdims=True)


def levels_of(sums, top):
    inverse = LEVELS / jnp.maximum(top, 1e-30)
    return jnp.round(sums * inverse).astype(I32).astype(I16)


def kernel(
    sizes,
    tiles_hbm,
    trow_hbm,
    tcol_hbm,
    count_ref,
    cost_hbm,
    upper_hbm,
    kind_hbm,
    rhs_hbm,
    rkind_hbm,
    primal_hbm,
    dual_hbm,
    out_ref,
    tiles,
    turned,
    raw_idx,
    col_vecs,
    col_kind,
    row_vecs,
    row_kind_full,
    idx_src,
    idx_x,
    idx_z,
    idx_y,
    idx_c,
    match_z,
    match_y,
    px_src,
    px_dst,
    zq_src,
    zq_dst,
    zs_src,
    zs_dst,
    zo_src,
    zo_dst,
    pc_src,
    pc_dst,
    yq_src,
    yq_dst,
    ys_src,
    ys_dst,
    yo_src,
    yo_dst,
    lq_src,
    ls_src,
    mid_src,
    mid_dst,
    po_src,
    po_dst,
    last_y,
    fin_src,
    fin_dst,
    load_sems,
    send_sems,
    recv_sems,
):
    n_x, n_z, n_y, n_core, slots = sizes
    n_row, n_col = n_x * n_z, n_y * n_core
    n_rblocks, n_cblocks = n_col * SHARE, n_row * SHARE
    me_row = lax.axis_index("row")
    me_col = lax.axis_index("col")
    my_x, my_z = lax.div(me_row, n_z), lax.rem(me_row, n_z)
    my_y, my_core = lax.div(me_col, n_core), lax.rem(me_col, n_core)

    def x_peer(step):
        at = lax.rem(my_x + zigzag(step, n_x), n_x)
        return at, (at * n_z + my_z, me_col)

    def z_peer(step):
        at = lax.rem(my_z + zigzag(step, n_z), n_z)
        return at, (my_x * n_z + at, me_col)

    def y_peer(step):
        at = lax.rem(my_y + zigzag(step, n_y), n_y)
        return at, (me_row, at * n_core + my_core)

    def core_peer(step):
        at = lax.rem(my_core + 1 + step, n_core)
        return at, (me_row, my_y * n_core + at)

    def last_peer(step):
        ahead = step // n_core
        to_z = lax.rem(my_z + zigzag(ahead // n_x, n_z), n_z)
        to_x = lax.rem(my_x + zigzag(ahead % n_x, n_x), n_x)
        to_core = lax.rem(my_core + n_core - 1 - step % n_core, n_core)
        return step, (to_x * n_z + to_z, my_y * n_core + to_core)

    n_last = n_row * n_core
    n_groups = slots // GROUP
    pieces = [pl.ds(g * GROUP, GROUP) for g in range(n_groups)]
    first_loads = [
        (trow_hbm, raw_idx.at[0]),
        (tcol_hbm, raw_idx.at[1]),
        (dual_hbm, row_vecs.at[0]),
    ]
    tile_loads = [(tiles_hbm.at[piece], tiles.at[piece]) for piece in pieces]
    late_loads = [
        (primal_hbm, col_vecs.at[0]),
        (cost_hbm, col_vecs.at[1]),
        (upper_hbm, col_vecs.at[2]),
        (kind_hbm, col_kind),
        (rhs_hbm, row_vecs.at[1]),
        (rkind_hbm, row_kind_full),
    ]
    copies = [
        pltpu.make_async_copy(src, dst, load_sems.at[i])
        for i, (src, dst) in enumerate(first_loads + tile_loads + late_loads)
    ]
    for copy in copies:
        copy.start()
    barrier = pltpu.get_barrier_semaphore()

    greeted = ((z_peer, n_z - 1), (y_peer, n_y - 1), (x_peer, n_x - 1), (core_peer, n_core - 1))
    for peer, count in greeted:

        @pl.loop(0, count)
        def _(step):
            pl.semaphore_signal(barrier, inc=1, device_id=peer(step)[1], device_id_type=MESH)

    n_first, n_tile = len(first_loads), len(tile_loads)
    for copy in copies[:n_first]:
        copy.wait()

    live = lax.broadcasted_iota(I32, (1, slots), 1) < count_ref[0, 0]
    block_rows = jnp.where(live, raw_idx[0], -1)
    block_cols = jnp.where(live, raw_idx[1], -1)
    row_pick = (
        (lax.broadcasted_iota(I32, (n_rblocks, slots), 0) == block_rows).astype(F32).T
    )
    sub = lax.broadcasted_iota(I32, (GROUP, TILE), 0)

    def spread(part):
        return jnp.concatenate(
            [jnp.where(sub == j, part, 0.0).astype(BF16) for j in range(GROUP)], axis=1
        )

    def back(part_of, ready):
        products = []
        for g in range(n_groups):
            ready(g)
            part = part_of[g * GROUP : (g + 1) * GROUP]
            block = tiles[g * GROUP : (g + 1) * GROUP].reshape(GROUP * TILE, TILE)
            products.append(jnp.dot(spread(part), block, preferred_element_type=F32))
        return jnp.concatenate(products, axis=0)

    def fore(part_of):
        products = []
        for g in range(n_groups):
            part = part_of[g * GROUP : (g + 1) * GROUP]
            block = turned[g * GROUP : (g + 1) * GROUP].reshape(GROUP * TILE, TILE)
            products.append(jnp.dot(spread(part), block, preferred_element_type=F32))
        return jnp.concatenate(products, axis=0)

    pending = []
    used = [0]

    def channel(peer, count, slot, *pairs):
        base = used[0]
        used[0] += len(pairs)

        def start(low, high):
            for step in range(low, high):
                device = peer(step)[1]
                for k, (source, dest) in enumerate(pairs):
                    pltpu.make_async_remote_copy(
                        src_ref=source(step),
                        dst_ref=dest.at[slot(step)],
                        send_sem=send_sems.at[base + k],
                        recv_sem=recv_sems.at[base + k],
                        device_id=device,
                        device_id_type=MESH,
                    ).start()

        started = [(dest.at[pl.ds(0, count)], base + k) for k, (_, dest) in enumerate(pairs)]
        pending.extend(started)

        def arrive():
            for both, sem in started:
                pltpu.make_async_copy(both, both, recv_sems.at[sem]).wait()

        return start, arrive

    def send(peer, count, slot, *pairs):
        start, arrive = channel(peer, count, slot, *pairs)
        start(0, count)
        return arrive

    def z_slot(step):
        return backward(n_z)[step]

    def y_slot(step):
        return backward(n_y)[step]

    def at_x(step):
        return my_x

    def at_y(step):
        return my_y

    def at_core(step):
        return my_core

    def put_split(ref, products):
        high = products.astype(BF16)
        ref[0:slots] = high
        ref[slots : 2 * slots] = (products - high.astype(F32)).astype(BF16)

    rounded = row_vecs[0].astype(BF16)
    picked = jnp.dot(row_pick.astype(BF16), rounded, preferred_element_type=F32)
    put_split(px_src.at[0], back(picked, lambda g: copies[n_first + g].wait()))
    idx_src[...] = jnp.full((2, TILE), -1, I32)
    idx_src[0:1, 0:slots] = block_cols
    idx_src[1:2, 0:slots] = block_rows
    pl.semaphore_wait(barrier, sum(count for _, count in greeted))

    z_idx_in = send(z_peer, n_z - 1, z_slot, (lambda step: idx_src, idx_z))
    x_idx_in = send(x_peer, n_x - 1, at_x, (lambda step: idx_src, idx_x))
    x_in = send(x_peer, n_x - 1, at_x, (lambda step: px_src.at[0], px_dst.at[0]))
    y_idx_in = send(y_peer, n_y - 1, y_slot, (lambda step: idx_src, idx_y))
    c_idx_in = send(core_peer, n_core - 1, at_core, (lambda step: idx_src, idx_c))
    for mine, ref in ((my_x, idx_x), (n_z - 1, idx_z), (n_y - 1, idx_y), (my_core, idx_c)):
        ref[mine] = idx_src[...]
    px_dst[0, my_x] = px_src[0]

    for copy in copies[n_first + n_tile :]:
        copy.wait()
    col_pick = (
        (lax.broadcasted_iota(I32, (n_cblocks, slots), 0) == block_cols).astype(F32).T
    )
    col_all = jnp.concatenate(
        [col_vecs[0], col_vecs[1], col_vecs[2], col_kind[...].astype(F32)], axis=1
    )
    col_got = jnp.dot(
        col_pick, col_all, precision=lax.Precision.HIGHEST, preferred_element_type=F32
    )
    x_need, cost_need, upper_need, kind_need = (
        col_got[:, i * TILE : (i + 1) * TILE] for i in range(4)
    )
    row_share = pl.ds(pl.multiple_of(me_row * SHARE, SHARE), SHARE)
    col_share = pl.ds(pl.multiple_of(me_col * SHARE, SHARE), SHARE)
    x_own, cost_own, upper_own = (col_vecs[i, row_share] for i in range(3))
    kind_own = col_kind[row_share]
    y_own, rhs_own, rkind_own = row_vecs[0, col_share], row_vecs[1, col_share], row_kind_full[col_share]

    z_idx_in()
    x_idx_in()
    need_cols = idx_z[:, 0, :].astype(F32).T[:slots]
    in_share = lax.broadcasted_iota(I32, (SHARE, TILE), 0)
    own_cols = jnp.concatenate(
        [in_share + (my_x * n_z + z_peer(step)[0]) * SHARE for step in range(n_z)], axis=0
    )
    for k in range(n_x):
        have = twice(idx_x[k, 0:1])
        lanes = slice(k * TILE, (k + 1) * TILE)
        have_wide = jnp.broadcast_to(have[0:1], (slots, TILE)).astype(F32)
        for z in range(n_z):
            match_z[z * slots : (z + 1) * slots, lanes] = jnp.where(
                need_cols[:, z : z + 1] == have_wide, 1.0, 0.0
            ).astype(BF16)
        match_z[n_z * slots :, lanes] = jnp.where(own_cols == have[0:1], 1.0, 0.0).astype(BF16)
    def total(levels, scales):
        return jnp.sum(levels.astype(F32) * scales, axis=0)

    n_zneed, n_yneed = n_z * slots, n_y * slots
    x_total = jnp.zeros_like(x_own)
    y_first = y_own
    for it in range(ITERS):
        last = it + 1 == ITERS
        x_in()
        parts = px_dst[it].reshape(n_x * 2 * slots, TILE)
        start, zq_in = channel(
            z_peer,
            n_z - 1,
            z_slot,
            (lambda step: zs_src.at[it, step], zs_dst.at[it]),
            (lambda step: zq_src.at[it, step], zq_dst.at[it]),
        )
        for low in range(0, n_z, n_z // CHUNKS):
            high = low + n_z // CHUNKS
            wanted = jnp.dot(
                match_z[low * slots : high * slots], parts, preferred_element_type=F32
            ).reshape(high - low, slots, TILE)
            top = lane_top(wanted)
            zs_src[it, low:high] = top * (1.0 / LEVELS)
            zq_src[it, low:high] = levels_of(wanted, top)
            start(low, min(high, n_z - 1))
        sums = jnp.dot(match_z[n_zneed:], parts, preferred_element_type=F32)
        zo_src[it] = sums.reshape(n_z, SHARE, TILE)
        if last:
            zo_in = send(z_peer, n_z - 1, z_slot, (lambda step: zo_src.at[it, step], zo_dst.at[it]))
        zq_dst[it, n_z - 1] = zq_src[it, n_z - 1]
        zs_dst[it, n_z - 1] = zs_src[it, n_z - 1]
        zo_dst[it, n_z - 1] = zo_src[it, n_z - 1]
        if it > 0:
            yo_in()
            y_first = project_dual(
                y_own + DUAL_STEP * (rhs_own - jnp.sum(yo_dst[...], axis=0)), rkind_own
            )
            mid_src[...] = y_first
            mid_in = send(y_peer, n_y - 1, at_y, (lambda step: mid_src, mid_dst))
            mid_dst[my_y] = y_first
        if it == 0:
            row_all = jnp.concatenate(
                [row_vecs[0], row_vecs[1], row_kind_full[...].astype(F32)], axis=1
            )
            row_got = jnp.dot(
                row_pick, row_all, precision=lax.Precision.HIGHEST, preferred_element_type=F32
            )
            y_need, rhs_need, rkind_need = (row_got[:, i * TILE : (i + 1) * TILE] for i in range(3))
            y_idx_in()
            c_idx_in()
            need_rows = idx_y[:, 1, :].astype(F32).T[:slots]
            own_rows = jnp.concatenate(
                [in_share + (y * n_core + my_core) * SHARE for y in range(n_y)], axis=0
            )
            for k in range(n_core):
                have = twice(idx_c[k, 1:2])
                lanes = slice(k * TILE, (k + 1) * TILE)
                have_wide = jnp.broadcast_to(have[0:1], (slots, TILE)).astype(F32)
                for y in range(n_y):
                    match_y[y * slots : (y + 1) * slots, lanes] = jnp.where(
                        need_rows[:, y : y + 1] == have_wide, 1.0, 0.0
                    ).astype(BF16)
                match_y[n_y * slots :, lanes] = jnp.where(own_rows == have[0:1], 1.0, 0.0).astype(BF16)

            @pl.loop(0, slots // 8)
            def _(part):
                for k in range(8):
                    turned[part * 8 + k] = tiles[part * 8 + k].T

        zq_in()
        x_new = project_primal(
            x_need - PRIMAL_STEP * (cost_need - total(zq_dst[it], zs_dst[it])),
            kind_need,
            upper_need,
        )
        if not last:
            zo_in = send(z_peer, n_z - 1, z_slot, (lambda step: zo_src.at[it, step], zo_dst.at[it]))
        put_split(pc_src.at[it], fore((2.0 * x_new - x_need).astype(BF16).astype(F32)))
        x_need = x_new
        c_in = send(core_peer, n_core - 1, at_core, (lambda step: pc_src.at[it], pc_dst.at[it]))
        pc_dst[it, my_core] = pc_src[it]
        if last:
            zo_in()
            x_own = project_primal(
                x_own - PRIMAL_STEP * (cost_own - jnp.sum(zo_dst[it], axis=0)), kind_own, upper_own
            )
            x_total = x_total + x_own
        c_in()
        parts = pc_dst[it].reshape(n_core * 2 * slots, TILE)
        if not last:
            start, yq_in = channel(
                y_peer,
                n_y - 1,
                y_slot,
                (lambda step: ys_src.at[step], ys_dst.at[it]),
                (lambda step: yq_src.at[step], yq_dst.at[it]),
            )
            for low in range(0, n_y, n_y // CHUNKS):
                high = low + n_y // CHUNKS
                wanted = jnp.dot(
                    match_y[low * slots : high * slots], parts, preferred_element_type=F32
                ).reshape(high - low, slots, TILE)
                top = lane_top(wanted)
                ys_src[low:high] = top * (1.0 / LEVELS)
                yq_src[low:high] = levels_of(wanted, top)
                start(low, min(high, n_y - 1))
            sums = jnp.dot(match_y[n_yneed:], parts, preferred_element_type=F32)
            yo_src[...] = sums.reshape(n_y, SHARE, TILE)
            yq_dst[it, n_y - 1] = yq_src[n_y - 1]
            ys_dst[it, n_y - 1] = ys_src[n_y - 1]
            yo_dst[n_y - 1] = yo_src[my_y]
            zo_in()
            x_own = project_primal(
                x_own - PRIMAL_STEP * (cost_own - jnp.sum(zo_dst[it], axis=0)), kind_own, upper_own
            )
            x_total = x_total + x_own
            yq_in()
            yo_in = send(y_peer, n_y - 1, y_slot, (lambda step: yo_src.at[y_peer(step)[0]], yo_dst))
            y_need = project_dual(
                y_need + DUAL_STEP * (rhs_need - total(yq_dst[it], ys_dst[it])), rkind_need
            )
            put_split(
                px_src.at[it + 1], back(y_need.astype(BF16).astype(F32), lambda g: None)
            )
            x_in = send(x_peer, n_x - 1, at_x, (lambda step: px_src.at[it + 1], px_dst.at[it + 1]))
            px_dst[it + 1, my_x] = px_src[it + 1]

    sums = jnp.dot(match_y[n_yneed:], parts, preferred_element_type=F32)
    top = lane_top(sums)
    ls_src[...] = top * (1.0 / LEVELS)
    lq_src[...] = levels_of(sums, top)
    yq_in = send(
        y_peer,
        n_y - 1,
        y_slot,
        (lambda step: ls_src, ys_dst.at[ITERS - 1]),
        (lambda step: lq_src, yq_dst.at[ITERS - 1]),
    )
    primal_avg = x_total / ITERS
    po_src[...] = jnp.sum(cost_own * primal_avg, axis=0, keepdims=True)
    po_in = send(y_peer, n_y - 1, y_slot, (lambda step: po_src, po_dst))
    yq_dst[ITERS - 1, n_y - 1] = lq_src[...]
    ys_dst[ITERS - 1, n_y - 1] = ls_src[...]
    po_dst[n_y - 1] = po_src[...]
    half_rhs = row_vecs[1].reshape(n_y, n_core, SHARE, TILE)
    half_kind = row_kind_full[...].reshape(n_y, n_core, SHARE, TILE)

    def of_core(both):
        one = both[:, 0]
        for k in range(1, n_core):
            one = jnp.where(my_core == k, both[:, k], one)
        return one.reshape(n_y * SHARE, TILE)

    half_rhs, half_kind = of_core(half_rhs), of_core(half_kind)
    mid_in()
    half_y = mid_dst[...].reshape(n_y * SHARE, TILE)
    po_in()
    fin_src[0:1] = jnp.sum(po_dst[...], axis=0)
    yq_in()
    half_new = project_dual(
        half_y + DUAL_STEP * (half_rhs - total(yq_dst[ITERS - 1], ys_dst[ITERS - 1])), half_kind
    )
    half_avg = (half_y + half_new) / ITERS
    fin_src[1:2] = jnp.sum(half_rhs * half_avg, axis=0, keepdims=True)
    me_last = me_row * n_core + my_core
    fin_in = send(last_peer, n_last - 1, lambda step: me_last, (lambda step: fin_src, fin_dst))
    fin_dst[me_last] = fin_src[...]
    last_y[0] = half_new
    last_y[1] = half_avg
    mine = pl.ds(pl.multiple_of(my_y * SHARE, SHARE), SHARE)
    out_ref[0] = x_own
    out_ref[1] = last_y[0, mine]
    out_ref[2] = primal_avg
    out_ref[3] = last_y[1, mine]
    for both, which in pending[:-1]:
        pltpu.make_async_copy(both, both, send_sems.at[which]).wait()
    fin_in()
    inner = jnp.sum(jnp.sum(fin_dst[...], axis=0), axis=1, keepdims=True)
    primal_scale = 1.0 / math.sqrt(n_cblocks * TILE * n_col)
    dual_scale = 1.0 / math.sqrt(n_rblocks * TILE * n_row)
    first = lax.broadcasted_iota(I32, (SHARE, TILE), 1) == 0
    out_ref[4] = jnp.where(first, inner[0:1] * primal_scale, inner[1:2] * dual_scale)
    both, which = pending[-1]
    pltpu.make_async_copy(both, both, send_sems.at[which]).wait()


def split_kernel(packed_ref, *out_refs):
    for i in range(4):
        out_refs[i][...] = packed_ref[i]
    out_refs[4][...] = packed_ref[4, 0:1, 0:2]


def solution(mesh):
    n_row, n_col = mesh.shape["row"], mesh.shape["col"]
    n_x, n_core = N_X, N_CORE
    n_z, n_y = n_row // n_x, n_col // n_core

    def body(
        tiles,
        tile_rows,
        tile_cols,
        tile_count,
        cost,
        upper,
        var_kind,
        rhs,
        row_kind,
        primal_start,
        dual_start,
    ):
        slots = tiles.shape[2]
        sizes = (n_x, n_z, n_y, n_core, slots)
        n_rblocks, n_cblocks = n_col * SHARE, n_row * SHARE
        n_last = n_row * n_core
        anywhere = pl.BlockSpec(memory_space=pl.ANY)
        vmem = pl.BlockSpec(memory_space=pltpu.VMEM)
        smem = pl.BlockSpec(memory_space=pltpu.SMEM)
        scratch = [
            ((slots, TILE, TILE), BF16),
            ((slots, TILE, TILE), BF16),
            ((2, 1, slots), I32),
            ((3, n_cblocks, TILE), F32),
            ((n_cblocks, TILE), I32),
            ((2, n_rblocks, TILE), F32),
            ((n_rblocks, TILE), I32),
            ((2, TILE), I32),
            ((n_x, 2, TILE), I32),
            ((n_z, 2, TILE), I32),
            ((n_y, 2, TILE), I32),
            ((n_core, 2, TILE), I32),
            ((n_z * (slots + SHARE), n_x * TILE), BF16),
            ((n_y * (slots + SHARE), n_core * TILE), BF16),
            ((ITERS, 2 * slots, TILE), BF16),
            ((ITERS, n_x, 2 * slots, TILE), BF16),
            ((ITERS, n_z, slots, TILE), I16),
            ((ITERS, n_z, slots, TILE), I16),
            ((ITERS, n_z, 1, TILE), F32),
            ((ITERS, n_z, 1, TILE), F32),
            ((ITERS, n_z, SHARE, TILE), F32),
            ((ITERS, n_z, SHARE, TILE), F32),
            ((ITERS, 2 * slots, TILE), BF16),
            ((ITERS, n_core, 2 * slots, TILE), BF16),
            ((n_y, slots, TILE), I16),
            ((ITERS, n_y, slots, TILE), I16),
            ((n_y, 1, TILE), F32),
            ((ITERS, n_y, 1, TILE), F32),
            ((n_y, SHARE, TILE), F32),
            ((n_y, SHARE, TILE), F32),
            ((n_y * SHARE, TILE), I16),
            ((1, TILE), F32),
            ((SHARE, TILE), F32),
            ((n_y, SHARE, TILE), F32),
            ((1, TILE), F32),
            ((n_y, 1, TILE), F32),
            ((2, n_y * SHARE, TILE), F32),
            ((2, TILE), F32),
            ((n_last, 2, TILE), F32),
        ]
        def in_hbm(array):
            return pltpu.with_memory_space_constraint(array, pltpu.HBM)

        packed = pl.pallas_call(
            functools.partial(kernel, sizes),
            out_shape=pltpu.VMEM((5, SHARE, TILE), F32),
            in_specs=[anywhere] * 3 + [smem] + [anywhere] * 7,
            out_specs=vmem,
            scratch_shapes=[pltpu.VMEM(shape, dtype) for shape, dtype in scratch]
            + [
                pltpu.SemaphoreType.DMA((9 + slots // GROUP,)),
                pltpu.SemaphoreType.DMA((SEMS,)),
                pltpu.SemaphoreType.DMA((SEMS,)),
            ],
            compiler_params=pltpu.CompilerParams(
                collective_id=0, has_side_effects=True, vmem_limit_bytes=48 * 2**20
            ),
            name="pdhg",
        )(
            in_hbm(tiles.reshape(slots, TILE, TILE)),
            in_hbm(tile_rows.reshape(1, slots)),
            in_hbm(tile_cols.reshape(1, slots)),
            tile_count,
            in_hbm(cost.reshape(n_cblocks, TILE)),
            in_hbm(upper.reshape(n_cblocks, TILE)),
            in_hbm(var_kind.reshape(n_cblocks, TILE)),
            in_hbm(rhs.reshape(n_rblocks, TILE)),
            in_hbm(row_kind.reshape(n_rblocks, TILE)),
            in_hbm(primal_start.reshape(n_cblocks, TILE)),
            in_hbm(dual_start.reshape(n_rblocks, TILE)),
        )
        share = jax.ShapeDtypeStruct((SHARE, TILE), F32)
        outs = pl.pallas_call(
            split_kernel,
            out_shape=(share,) * 4 + (jax.ShapeDtypeStruct((1, 2), F32),),
            in_specs=[vmem],
            out_specs=(vmem,) * 5,
            name="unpack",
        )(pltpu.with_memory_space_constraint(packed, pltpu.VMEM))
        return tuple(o.reshape(-1) for o in outs)

    placed = (
        P("row", "col", None, None, None),
        P("row", "col", None),
        P("row", "col", None),
        P("row", "col"),
        P("col"),
        P("col"),
        P("col"),
        P("row"),
        P("row"),
        P("col"),
        P("row"),
    )
    return jax.shard_map(
        body,
        mesh=mesh,
        in_specs=placed,
        out_specs=(P(("col", "row")), P(("row", "col")), P(("col", "row")), P(("row", "col")), P()),
        check_vma=False,
    )
```
